512 devices in a mesh: clip: 32 (over x_hi, z), frame: 16 (over y, x_lo, core).
Axes of the slice: x: 4 (x_hi: 2, x_lo: 2; x = x_hi * 2 + x_lo), y: 4, z: 16, core: 2. Of those that a mesh axis runs over, the one named last changes fastest.
Arguments:
- clips: bfloat16 [32, 16, 16, 32, 256], P('clip', 'frame'), may hold values from -25 to 25, as said below
- cotangent: bfloat16 [32, 16, 16, 32, 256], P('clip', 'frame'), may hold values from -25 to 25
- norm_gain: float32 [256], replicated, may hold values from 0.25 to 1.75
- norm_shift: float32 [256], replicated, may hold values from -3 to 3
- w_spatial: bfloat16 [3, 3, 256, 256], replicated, may hold values from -0.125 to 0.125
- w_time: bfloat16 [3, 256, 256], replicated, may hold values from -0.21875 to 0.21875
Outputs:
- result_video: bfloat16 [32, 16, 16, 32, 256], P('clip', 'frame')
- input_grad: bfloat16 [32, 16, 16, 32, 256], P('clip', 'frame')
- spatial_grad: bfloat16 [3, 3, 256, 256], P(None, None, 'frame')
- time_grad: bfloat16 [3, 256, 256], P(None, 'frame')
The draws below stay inside these ranges and needn't reach their ends.
Inputs may be any that keep to these rules, and one draw needn't show every extreme that they name: `clips`: input activations.
All inputs are finite; a program needn't handle non-finite values.
Results may differ from the reference program's by a relative error of at most 0.0029.
Values may be sent and summed in bfloat16 or wider, within the bound.
A program may use at most 64 MiB of HBM per device.

```python
import math
import jax
import jax.numpy as jnp
from jax import lax

C = 256
GROUPS = 32
HH = 16
WW = 32
CLIPS = 32
FRAMES = 16


def draw_clips(key, part):
    key = jax.random.fold_in(key, 7)
    base_key, rough_key, offset_key, sign_key, level_key = jax.random.split(key, 5)
    full_shape = (CLIPS, FRAMES, HH, WW, C)
    position = jnp.arange(FRAMES, dtype=jnp.float32) / max(FRAMES - 1, 1)
    base_values = jnp.clip(jax.random.normal(base_key, full_shape, jnp.float32), -4.0, 4.0)
    frame_ramp = 1.0 + 2.0 * position
    level = jax.random.uniform(level_key, (CLIPS, GROUPS), jnp.float32, 0.5, 1.0)
    signs = jnp.where(jax.random.randint(sign_key, (CLIPS, GROUPS), 0, 2) == 0, -1.0, 1.0)
    group_level = jnp.repeat(signs * level, C // GROUPS, axis=1)
    drift = 3.0 * (2.0 * position - 1.0)
    frame_drift = drift[None, :, None, None, None] * group_level[:, None, None, None, :]
    roughness = jax.random.uniform(rough_key, (CLIPS, FRAMES, HH, WW, 1), jnp.float32, 0.5, 1.5)
    offset = 0.5 * jnp.clip(jax.random.normal(offset_key, (CLIPS, FRAMES, 1, 1, C), jnp.float32), -3.0, 3.0)
    return (base_values * roughness * frame_ramp[None, :, None, None, None] + offset + frame_drift).astype(jnp.bfloat16)


def draw_cotangent(key, part):
    key = jax.random.fold_in(key, 11)
    base_key, common_key = jax.random.split(key, 2)
    full_shape = (CLIPS, FRAMES, HH, WW, C)
    position = jnp.arange(FRAMES, dtype=jnp.float32) / max(FRAMES - 1, 1)
    base_values = jnp.clip(jax.random.normal(base_key, full_shape, jnp.float32), -4.0, 4.0)
    frame_ramp = 1.0 + 2.0 * position
    common_part = jnp.clip(jax.random.normal(common_key, (CLIPS, 1, 1, 1, C), jnp.float32), -2.5, 2.5)
    swing = 8.0 * (position - 0.5)
    return (base_values * frame_ramp[None, :, None, None, None] + common_part * swing[None, :, None, None, None]).astype(jnp.bfloat16)


def scatter_about(own_key, extent, deviation, most, kind=jnp.bfloat16):
    array = jax.random.normal(own_key, extent, jnp.float32) * deviation
    return jnp.minimum(jnp.maximum(array, -most), most).astype(kind)


def setup_inputs(seed: int = 0) -> dict:
    splits = jax.random.split(jax.random.key(seed), 7)
    return {
        "clips": draw_clips(jax.random.fold_in(splits[6], 71), 0),
        "cotangent": draw_cotangent(jax.random.fold_in(splits[6], 71), 0),
        "norm_gain": jnp.clip(1.0 + 0.15 * jax.random.normal(splits[2], (C,), jnp.float32), 0.25, 1.75),
        "norm_shift": scatter_about(splits[3], (C,), 0.5, 3.0, jnp.float32),
        "w_spatial": scatter_about(splits[4], (3, 3, C, C), (9 * C) ** -0.5, 0.125),
        "w_time": scatter_about(splits[5], (3, C, C), (3 * C) ** -0.5, 0.21875),
    }


epsilon = 1e-05

def group_sums(values, groups):
    return values.reshape(groups, -1).sum(axis=1)

def spread_groups(values, channels):
    return jnp.repeat(values, channels // values.shape[0])

def spatial_conv(hidden, weights):
    row_count, col_count, channels = (hidden.shape[1], hidden.shape[2], hidden.shape[3])
    padded = jnp.pad(hidden, ((0, 0), (1, 1), (1, 1), (0, 0)))
    running = jnp.zeros((hidden.shape[0] * row_count * col_count, weights.shape[-1]), jnp.float32)
    for row_tap in range(3):
        for col_tap in range(3):
            window = padded[:, row_tap:row_tap + row_count, col_tap:col_tap + col_count, :].reshape(-1, channels)
            running = running + jnp.dot(window, weights[row_tap, col_tap], preferred_element_type=jnp.float32)
    return running.reshape(hidden.shape[:-1] + (weights.shape[-1],))

def spatial_weights(hidden, gradient):
    row_count, col_count, channels = (hidden.shape[1], hidden.shape[2], hidden.shape[3])
    padded = jnp.pad(hidden, ((0, 0), (1, 1), (1, 1), (0, 0)))
    flat_grad = gradient.reshape(-1, gradient.shape[-1])
    rows_out = []
    for row_tap in range(3):
        cols_out = []
        for col_tap in range(3):
            window = padded[:, row_tap:row_tap + row_count, col_tap:col_tap + col_count, :].reshape(-1, channels)
            cols_out.append(jnp.dot(window.T, flat_grad, preferred_element_type=jnp.float32))
        rows_out.append(jnp.stack(cols_out))
    return jnp.stack(rows_out)

def causal_conv(sequence, w_time):
    frames, channels = (sequence.shape[0], sequence.shape[-1])
    padded = jnp.pad(sequence, ((2, 0),) + ((0, 0),) * (sequence.ndim - 1))
    running = jnp.zeros((sequence.size // channels, channels), jnp.float32)
    for offset in range(3):
        running = running + jnp.dot(padded[2 - offset:2 - offset + frames].reshape(-1, channels), w_time[offset], preferred_element_type=jnp.float32)
    return running.reshape(sequence.shape)

def causal_back(gradient, w_time):
    frames, channels = (gradient.shape[0], gradient.shape[-1])
    padded = jnp.pad(gradient, ((0, 2),) + ((0, 0),) * (gradient.ndim - 1))
    running = jnp.zeros((gradient.size // channels, channels), jnp.float32)
    for offset in range(3):
        running = running + jnp.dot(padded[offset:offset + frames].reshape(-1, channels), w_time[offset].T, preferred_element_type=jnp.float32)
    return running.reshape(gradient.shape)

def causal_weights(sequence, gradient):
    frames, channels = (sequence.shape[0], sequence.shape[-1])
    padded = jnp.pad(sequence, ((2, 0),) + ((0, 0),) * (sequence.ndim - 1))
    flat_grad = gradient.reshape(-1, channels)
    return jnp.stack([jnp.dot(padded[2 - offset:2 - offset + frames].reshape(-1, channels).T, flat_grad, preferred_element_type=jnp.float32) for offset in range(3)])

def reference(clips, cotangent, norm_gain, norm_shift, w_spatial, w_time):
    flipped = jnp.swapaxes(w_spatial[::-1, ::-1], 2, 3)
    members = FRAMES * HH * WW * (C // GROUPS)

    def one_clip(carry, pair):
        video_clip, gradient = pair
        values = video_clip.astype(jnp.float32)
        center = group_sums(lax.optimization_barrier(jnp.sum(values, axis=(0, 1, 2))), GROUPS) / members
        centered = values - spread_groups(center, C)
        variance = group_sums(lax.optimization_barrier(jnp.sum(centered * centered, axis=(0, 1, 2))), GROUPS) / members
        inv_std = lax.rsqrt(variance + epsilon)
        normed = centered * spread_groups(inv_std, C)
        activation = normed * norm_gain + norm_shift
        hidden = jax.nn.silu(activation).astype(jnp.bfloat16)
        mixed = spatial_conv(hidden, w_spatial).astype(jnp.bfloat16)
        temporal = causal_conv(mixed, w_time).astype(jnp.bfloat16)
        result_video = (values + temporal.astype(jnp.float32)).astype(jnp.bfloat16)
        mixed_grad = causal_back(gradient, w_time).astype(jnp.bfloat16)
        time_part = causal_weights(mixed, gradient)
        spatial_part = spatial_weights(hidden, mixed_grad)
        hidden_grad = spatial_conv(mixed_grad, flipped)
        sigmoid_act = jax.nn.sigmoid(activation)
        act_grad = hidden_grad * sigmoid_act * (1.0 + activation * (1.0 - sigmoid_act))
        normed_grad = act_grad * norm_gain
        first_mean = group_sums(lax.optimization_barrier(jnp.sum(normed_grad, axis=(0, 1, 2))), GROUPS) / members
        second_mean = group_sums(lax.optimization_barrier(jnp.sum(normed_grad * normed, axis=(0, 1, 2))), GROUPS) / members
        input_grad = gradient.astype(jnp.float32) + spread_groups(inv_std, C) * (normed_grad - spread_groups(first_mean, C) - normed * spread_groups(second_mean, C))
        return ((carry[0] + spatial_part, carry[1] + time_part), (result_video, input_grad.astype(jnp.bfloat16)))
    start = (jnp.zeros((3, 3, C, C), jnp.float32), jnp.zeros((3, C, C), jnp.float32))
    (spatial_sum, time_sum), (result_video, input_grad) = lax.scan(one_clip, start, (clips, cotangent))
    grad_scale = 1.0 / math.sqrt(CLIPS * FRAMES * HH * WW)
    return (result_video, input_grad, (spatial_sum * grad_scale).astype(jnp.bfloat16), (time_sum * grad_scale).astype(jnp.bfloat16))
```

```python
import functools
import math

import jax
import jax.numpy as jnp
from jax import lax
from jax.experimental import pallas as pl
from jax.experimental.pallas import tpu as pltpu
from jax.sharding import PartitionSpec as P

GROUPS = 32
EPSILON = 1e-05
MESH = pl.DeviceIdType.MESH
F32 = jnp.float32
BF16 = jnp.bfloat16

ROWS, COLS, C = 16, 32, 256
POS = ROWS * COLS
PAD = COLS
TAPS = 12
CHUNKS = 4
PIECE = POS // CHUNKS

ZS, XH, CHIPS = 16, 2, 8
FRAMES = 2 * CHIPS


def dot(a, b):
    return jnp.dot(a, b, preferred_element_type=F32)


def remote(src, dst, send_sem, recv_sem, clip, frame):
    return pltpu.make_async_remote_copy(
        src_ref=src,
        dst_ref=dst,
        send_sem=send_sem,
        recv_sem=recv_sem,
        device_id=(clip, frame),
        device_id_type=MESH,
    )


def wait_for(ref, sem):
    pltpu.make_async_copy(ref, ref, sem).wait()


def loop(count, body):
    def step(i, carry):
        body(i)
        return carry

    lax.fori_loop(0, count, step, 0)


def group_spread(row):
    lane = lax.broadcasted_iota(jnp.int32, row.shape, 1)
    for bit in (1, 2, 4):
        up = pltpu.roll(row, bit, 1)
        down = pltpu.roll(row, row.shape[1] - bit, 1)
        row = row + jnp.where((lane & bit) != 0, up, down)
    return row


def shifted(values, by, column):
    if by == 0:
        return values
    rolled = pltpu.roll(values, (-by) % values.shape[0], 0)
    edge = 0 if by < 0 else COLS - 1
    return jnp.where(column == edge, 0.0, rolled)


def by_parity(columns):
    strips = columns.reshape(8, 2, 16, columns.shape[1])
    return (
        strips[:, 0].reshape(128, columns.shape[1]),
        strips[:, 1].reshape(128, columns.shape[1]),
    )


def kernel(
    clips, cot, gain, shift, w_space, w_time,
    result_out, grad_out, space_out, time_out,
    clips_v, cot4, w_space_v, w_time_v, w_space_t, w_time_t,
    hcat, mgcat, act_s, ng_s, h_t, h_tx, m_t, m_tx, mixed_own, mixed_halo, mixed_sib,
    stat_tx, stat_rx, mean_tx, mean_rx,
    rs_tx_a, rs_rx_a, rs_tx_b, rs_rx_b, z_tx, z_rx, fin_tx, gathered,
    local_sem, send_sem, recv_sem, piece_sem,
):
    clip = lax.axis_index("clip")
    frame = lax.axis_index("frame")
    xh, z = clip // ZS, lax.rem(clip, ZS)
    q, core = frame // 2, lax.rem(frame, 2)
    sibling = frame + 1 - 2 * core
    members = FRAMES * POS * (C // GROUPS)

    copies = [
        pltpu.make_async_copy(clips, clips_v, local_sem.at[0]),
        pltpu.make_async_copy(w_time, w_time_v, local_sem.at[1]),
        pltpu.make_async_copy(w_space, w_space_v, local_sem.at[2]),
        pltpu.make_async_copy(cot, cot4.at[core], local_sem.at[3]),
    ]
    for copy in copies:
        copy.start()

    barrier = pltpu.get_barrier_semaphore()

    def greet(clip_to, frame_to):
        pl.semaphore_signal(
            barrier, inc=1, device_id=(clip_to, frame_to), device_id_type=MESH
        )

    def greet_line(i):
        greet(lax.rem(clip + i + 1, XH * ZS), frame)

    def greet_frame(i):
        greet(clip, lax.rem(frame + i + 1, FRAMES))

    def greet_plane(i):
        greet((1 - xh) * ZS + z, lax.rem(frame + 2 * (i + 1), FRAMES))

    loop(XH * ZS - 1, greet_line)
    loop(FRAMES - 1, greet_frame)
    loop(CHIPS - 1, greet_plane)

    zero = jnp.zeros((PAD, 3 * C), BF16)
    for buffer in (hcat, mgcat.at[0], mgcat.at[1]):
        buffer[0:PAD, :] = zero
        buffer[PAD + POS : PAD + POS + PAD, :] = zero

    copies[0].wait()
    values = clips_v[...].astype(F32)
    own_sum = group_spread(jnp.sum(values, axis=0, keepdims=True))
    own_mean = own_sum / (POS * (C // GROUPS))
    offset = values - own_mean
    own_squares = group_spread(jnp.sum(offset * offset, axis=0, keepdims=True))
    stat_tx[:, 0:C] = own_sum
    stat_tx[:, C : 2 * C] = own_squares
    copies[1].wait()
    for k in range(3):
        w_time_t[k] = w_time_v[k].T
    copies[2].wait()
    for p in range(3):
        for j in range(3):
            w_space_t[p, j * C : (j + 1) * C, :] = w_space_v[p, j * C : (j + 1) * C, :].T

    pl.semaphore_wait(barrier, XH * ZS - 1 + FRAMES - 1 + CHIPS - 1)

    def share_stats(i):
        remote(
            stat_tx, stat_rx.at[i], send_sem.at[0], recv_sem.at[0],
            clip, lax.rem(frame + i + 1, FRAMES),
        ).start()

    loop(FRAMES - 1, share_stats)

    before = lax.rem(frame + FRAMES - 2, FRAMES)
    after = lax.rem(frame + 2, FRAMES)
    for n in range(CHUNKS):
        rows = pl.ds(n * PIECE, PIECE)
        remote(
            cot.at[rows], cot4.at[2 + core, rows], send_sem.at[1], piece_sem.at[n], clip, before
        ).start()
    remote(cot, cot4.at[core], send_sem.at[2], recv_sem.at[2], clip, sibling).start()

    wait_for(stat_rx, recv_sem.at[0])
    own = stat_tx[...]
    sums = own[:, 0:C]
    squares = own[:, C : 2 * C]
    for i in range(FRAMES - 1):
        sums = sums + stat_rx[i, :, 0:C]
        squares = squares + stat_rx[i, :, C : 2 * C]
    center = sums / members
    part = POS * (C // GROUPS)
    away = own[:, 0:C] / part - center
    spread = away * away
    for i in range(FRAMES - 1):
        away = stat_rx[i, :, 0:C] / part - center
        spread = spread + away * away
    variance = (squares + part * spread) / members
    inv_std = lax.rsqrt(variance + EPSILON)

    column = lax.rem(lax.broadcasted_iota(jnp.int32, (POS, C), 0), COLS)
    normed = (clips_v[...].astype(F32) - center) * inv_std
    act = normed * gain[...] + shift[...]
    act_s[...] = act
    hidden = act / (1.0 + jnp.exp(-act))
    for j in range(3):
        hcat[PAD : PAD + POS, j * C : (j + 1) * C] = shifted(hidden, j - 1, column).astype(BF16)
    even, odd = by_parity(hidden.astype(BF16).T)
    first = core == 0
    h_tx[...] = jnp.where(first, odd, even)
    h_t[core] = jnp.where(first, even, odd)
    remote(h_tx, h_t.at[core], send_sem.at[3], recv_sem.at[3], clip, sibling).start()

    for n in range(CHUNKS):
        rows = pl.ds(n * PIECE, PIECE)
        wait_for(cot4.at[2 + core, rows], piece_sem.at[n])
        remote(
            cot4.at[2 + core, rows], cot4.at[2 + core, rows],
            send_sem.at[4], recv_sem.at[4], clip, sibling,
        ).start()

    mixed = dot(hcat[0:POS, :], w_space_v[0])
    for p in range(1, 3):
        mixed = mixed + dot(hcat[p * COLS : p * COLS + POS, :], w_space_v[p])
    mixed = mixed.astype(BF16)
    mixed_own[...] = mixed
    even, odd = by_parity(mixed.T)
    m_tx[...] = jnp.where(first, odd, even)
    m_t[core] = jnp.where(first, even, odd)
    remote(m_tx, m_t.at[core], send_sem.at[5], recv_sem.at[5], clip, sibling).start()

    copies[3].wait()
    wait_for(cot4.at[0], recv_sem.at[2])
    wait_for(cot4.at[0], recv_sem.at[4])
    wait_for(cot4.at[0], send_sem.at[4])

    @pl.when(q == CHIPS - 1)
    def _():
        cot4[2] = jnp.zeros((POS, C), BF16)
        cot4[3] = jnp.zeros((POS, C), BF16)

    for a in range(2):
        mg = dot(cot4[a], w_time_t[0]) + dot(cot4[a + 1], w_time_t[1])
        mg = mg + dot(cot4[a + 2], w_time_t[2])
        mg = mg.astype(BF16).astype(F32)
        for j in range(3):
            mgcat[a, PAD : PAD + POS, j * C : (j + 1) * C] = shifted(mg, 1 - j, column).astype(BF16)

    wait_for(h_t.at[0], recv_sem.at[3])
    for p in range(3):
        rows = pl.ds((2 - p) * COLS, POS)
        total = dot(h_t[0], mgcat[0, rows, :]) + dot(h_t[1], mgcat[1, rows, :])
        total = total.astype(BF16)
        for half in range(2):
            for to in range(CHIPS):
                for j in range(3):
                    rs_tx_a[half * CHIPS + to, 3 * p + j] = total[
                        to * 16 : to * 16 + 16, j * C + half * 128 : j * C + half * 128 + 128
                    ]

    def plane_target(i):
        r = i + 1
        xh_to = lax.rem(xh + r // CHIPS, XH)
        q_to = lax.rem(q + lax.rem(r, CHIPS), CHIPS)
        return xh_to * CHIPS + q_to, xh_to * ZS + z, 2 * q_to + core

    def scatter_a(i):
        to, clip_to, frame_to = plane_target(i)
        remote(
            rs_tx_a.at[to], rs_rx_a.at[i], send_sem.at[6], recv_sem.at[6], clip_to, frame_to
        ).start()

    loop(XH * CHIPS - 1, scatter_a)

    wait_for(m_t.at[0], recv_sem.at[5])
    for k in range(3):
        total = (dot(m_t[0], cot4[k]) + dot(m_t[1], cot4[k + 1])).astype(BF16)
        for half in range(2):
            for to in range(CHIPS):
                rs_tx_b[half * CHIPS + to, k] = total[
                    to * 16 : to * 16 + 16, half * 128 : half * 128 + 128
                ]

    def scatter_b(i):
        to, clip_to, frame_to = plane_target(i)
        remote(
            rs_tx_b.at[to], rs_rx_b.at[i], send_sem.at[7], recv_sem.at[7], clip_to, frame_to
        ).start()

    loop(XH * CHIPS - 1, scatter_b)

    remote(mixed_own, mixed_halo, send_sem.at[8], recv_sem.at[8], clip, after).start()

    hidden_grad = dot(mgcat[core, 2 * COLS : 2 * COLS + POS, :], w_space_t[0])
    for p in range(1, 3):
        rows = pl.ds((2 - p) * COLS, POS)
        hidden_grad = hidden_grad + dot(mgcat[core, rows, :], w_space_t[p])
    act = act_s[...]
    s = 1.0 / (1.0 + jnp.exp(-act))
    ng = hidden_grad * s * (1.0 + act * (1.0 - s)) * gain[...]
    ng_s[...] = ng
    normed = (clips_v[...].astype(F32) - center) * inv_std
    mean_tx[:, 0:C] = group_spread(jnp.sum(ng, axis=0, keepdims=True))
    mean_tx[:, C : 2 * C] = group_spread(jnp.sum(ng * normed, axis=0, keepdims=True))

    def share_means(i):
        remote(
            mean_tx, mean_rx.at[i], send_sem.at[9], recv_sem.at[9],
            clip, lax.rem(frame + i + 1, FRAMES),
        ).start()

    loop(FRAMES - 1, share_means)

    me = xh * CHIPS + q

    def along_z(k):
        @pl.when(k != z)
        def _():
            remote(
                z_tx.at[k], z_rx.at[lax.rem(z - k + ZS, ZS) - 1],
                send_sem.at[10], recv_sem.at[10], xh * ZS + k, frame,
            ).start()

    wait_for(rs_rx_a, recv_sem.at[6])
    for k in range(9):
        total = rs_tx_a[me, k].astype(F32)
        for i in range(XH * CHIPS - 1):
            total = total + rs_rx_a[i, k].astype(F32)
        z_tx[k] = total
    loop(9, along_z)
    wait_for(rs_rx_b, recv_sem.at[7])
    for k in range(3):
        total = rs_tx_b[me, k].astype(F32)
        for i in range(XH * CHIPS - 1):
            total = total + rs_rx_b[i, k].astype(F32)
        z_tx[9 + k] = total
    loop(3, lambda i: along_z(i + 9))

    wait_for(mean_rx, recv_sem.at[9])
    both = mean_tx[...]
    for i in range(FRAMES - 1):
        both = both + mean_rx[i]
    both = both / members
    m1, m2 = both[:, 0:C], both[:, C : 2 * C]
    normed = (clips_v[...].astype(F32) - center) * inv_std
    grad_out[...] = (
        cot4[core].astype(F32) + inv_std * (ng_s[...] - m1 - normed * m2)
    ).astype(BF16)

    wait_for(mixed_halo, recv_sem.at[8])

    @pl.when(core == 0)
    def _():
        remote(mixed_own, mixed_sib, send_sem.at[11], recv_sem.at[11], clip, sibling).start()

    @pl.when(core == 1)
    def _():
        remote(mixed_halo, mixed_sib, send_sem.at[11], recv_sem.at[11], clip, sibling).start()

    temporal = dot(mixed_own[...], w_time_v[0])
    temporal = temporal + jnp.where(q > 0, dot(mixed_halo[...], w_time_v[2]), 0.0)
    wait_for(mixed_sib, recv_sem.at[11])
    temporal = temporal + jnp.where(frame > 0, dot(mixed_sib[...], w_time_v[1]), 0.0)
    result_out[...] = (clips_v[...].astype(F32) + temporal.astype(BF16).astype(F32)).astype(BF16)

    scale = 1.0 / math.sqrt(XH * ZS * FRAMES * POS)

    @pl.when(z < TAPS)
    def _():
        wait_for(z_rx, recv_sem.at[10])
        total = z_tx[z]
        for i in range(ZS - 1):
            total = total + z_rx[i]
        done = (total * scale).astype(BF16)
        fin_tx[...] = done
        gathered[z * 2 + xh] = done

        def hand_out(i):
            remote(
                fin_tx, gathered.at[z * 2 + xh], send_sem.at[12], recv_sem.at[12],
                lax.rem(clip + i + 1, XH * ZS), frame,
            ).start()

        loop(XH * ZS - 1, hand_out)
        wait_for(gathered.at[pl.ds(0, 2 * TAPS - 1)], recv_sem.at[12])
        wait_for(gathered.at[pl.ds(0, XH * ZS - 1)], send_sem.at[12])
        wait_for(z_tx.at[pl.ds(0, TAPS - 1)], send_sem.at[10])

    @pl.when(z >= TAPS)
    def _():
        wait_for(gathered.at[pl.ds(0, 2 * TAPS)], recv_sem.at[12])
        wait_for(z_tx, send_sem.at[10])

    for k in range(TAPS):
        out = space_out.at[k] if k < 9 else time_out.at[k - 9]
        for half in range(2):
            out[:, half * 128 : half * 128 + 128] = gathered[2 * k + half]

    wait_for(stat_rx, send_sem.at[0])
    wait_for(cot4.at[0], send_sem.at[1])
    wait_for(cot4.at[0], send_sem.at[2])
    wait_for(h_tx, send_sem.at[3])
    wait_for(m_tx, send_sem.at[5])
    wait_for(rs_rx_a, send_sem.at[6])
    wait_for(rs_rx_b, send_sem.at[7])
    wait_for(mixed_own, send_sem.at[8])
    wait_for(mean_rx, send_sem.at[9])
    wait_for(mixed_own, send_sem.at[11])


def per_device(clips, cotangent, norm_gain, norm_shift, w_spatial, w_time):
    anywhere = pl.BlockSpec(memory_space=pl.ANY)
    vmem = pl.BlockSpec(memory_space=pltpu.VMEM)
    result, grad, space, time = pl.pallas_call(
        kernel,
        name="video_block",
        out_shape=(
            jax.ShapeDtypeStruct((POS, C), BF16),
            jax.ShapeDtypeStruct((POS, C), BF16),
            jax.ShapeDtypeStruct((9, 16, C), BF16),
            jax.ShapeDtypeStruct((3, 16, C), BF16),
        ),
        in_specs=[anywhere, anywhere, vmem, vmem, anywhere, anywhere],
        out_specs=(vmem, vmem, vmem, vmem),
        scratch_shapes=[
            pltpu.VMEM((POS, C), BF16),
            pltpu.VMEM((4, POS, C), BF16),
            pltpu.VMEM((3, 3 * C, C), BF16),
            pltpu.VMEM((3, C, C), BF16),
            pltpu.VMEM((3, 3 * C, C), BF16),
            pltpu.VMEM((3, C, C), BF16),
            pltpu.VMEM((POS + 2 * PAD, 3 * C), BF16),
            pltpu.VMEM((2, POS + 2 * PAD, 3 * C), BF16),
            pltpu.VMEM((POS, C), F32),
            pltpu.VMEM((POS, C), F32),
            pltpu.VMEM((2, 128, POS), BF16),
            pltpu.VMEM((128, POS), BF16),
            pltpu.VMEM((2, 128, POS), BF16),
            pltpu.VMEM((128, POS), BF16),
            pltpu.VMEM((POS, C), BF16),
            pltpu.VMEM((POS, C), BF16),
            pltpu.VMEM((POS, C), BF16),
            pltpu.VMEM((1, 2 * C), F32),
            pltpu.VMEM((FRAMES - 1, 1, 2 * C), F32),
            pltpu.VMEM((1, 2 * C), F32),
            pltpu.VMEM((FRAMES - 1, 1, 2 * C), F32),
            pltpu.VMEM((XH * CHIPS, 9, 16, 128), BF16),
            pltpu.VMEM((XH * CHIPS - 1, 9, 16, 128), BF16),
            pltpu.VMEM((XH * CHIPS, 3, 16, 128), BF16),
            pltpu.VMEM((XH * CHIPS - 1, 3, 16, 128), BF16),
            pltpu.VMEM((TAPS, 16, 128), F32),
            pltpu.VMEM((ZS - 1, 16, 128), F32),
            pltpu.VMEM((16, 128), BF16),
            pltpu.VMEM((XH * ZS - 1, 16, 128), BF16),
            pltpu.SemaphoreType.DMA((4,)),
            pltpu.SemaphoreType.DMA((13,)),
            pltpu.SemaphoreType.DMA((13,)),
            pltpu.SemaphoreType.DMA((CHUNKS,)),
        ],
        compiler_params=pltpu.CompilerParams(
            collective_id=0, has_side_effects=True, vmem_limit_bytes=40 * 2**20
        ),
    )(
        clips.reshape(POS, C),
        cotangent.reshape(POS, C),
        norm_gain.reshape(1, C),
        norm_shift.reshape(1, C),
        w_spatial.reshape(3, 3 * C, C),
        w_time,
    )
    return (
        result.reshape(clips.shape),
        grad.reshape(clips.shape),
        space.reshape(3, 3, 16, C),
        time,
    )


def solution(mesh):
    placed = (
        P("clip", "frame", None, None, None),
        P("clip", "frame", None, None, None),
        P(),
        P(),
        P(),
        P(),
    )
    return jax.shard_map(
        per_device,
        mesh=mesh,
        in_specs=placed,
        out_specs=(
            P("clip", "frame", None, None, None),
            P("clip", "frame", None, None, None),
            P(None, None, "frame", None),
            P(None, "frame", None),
        ),
        check_vma=False,
    )
```

```python
import functools
import math

import jax
import jax.numpy as jnp
from jax import lax
from jax.experimental import pallas as pl
from jax.experimental.pallas import tpu as pltpu
from jax.sharding import PartitionSpec as P

GROUPS = 32
EPSILON = 1e-05
MESH = pl.DeviceIdType.MESH
F32 = jnp.float32
BF16 = jnp.bfloat16

ROWS, COLS, C = 16, 32, 256
POS = ROWS * COLS
PAD = COLS
TAPS = 12
VMEM_BYTES = 60 * 2**20

PLANE_ORDER = (
    (2, 2), (1, 0), (0, 1), (2, 1), (0, 3), (3, 0), (1, 2), (1, 1),
    (2, 3), (3, 3), (3, 2), (0, 2), (2, 0), (3, 1), (1, 3),
)
CHUNKS = 4
PIECE = POS // CHUNKS

ZS, XH, CHIPS = 16, 2, 8
FRAMES = 2 * CHIPS


def dot(a, b):
    return jnp.dot(a, b, preferred_element_type=F32)


def remote(src, dst, send_sem, recv_sem, clip, frame):
    return pltpu.make_async_remote_copy(
        src_ref=src,
        dst_ref=dst,
        send_sem=send_sem,
        recv_sem=recv_sem,
        device_id=(clip, frame),
        device_id_type=MESH,
    )


def wait_for(ref, sem):
    pltpu.make_async_copy(ref, ref, sem).wait()


def loop(count, body):
    def step(i, carry):
        body(i)
        return carry

    lax.fori_loop(0, count, step, 0)


def far_first(i):
    return ZS // 2 + ((i + 1) // 2) * (1 - 2 * lax.rem(i, 2))


def group_spread(row):
    lane = lax.broadcasted_iota(jnp.int32, row.shape, 1)
    for bit in (1, 2, 4):
        up = pltpu.roll(row, bit, 1)
        down = pltpu.roll(row, row.shape[1] - bit, 1)
        row = row + jnp.where((lane & bit) != 0, up, down)
    return row


def shifted(values, by, column):
    if by == 0:
        return values
    rolled = pltpu.roll(values, (-by) % values.shape[0], 0)
    edge = 0 if by < 0 else COLS - 1
    return jnp.where(column == edge, 0.0, rolled)


def by_parity(columns):
    strips = columns.reshape(8, 2, 16, columns.shape[1])
    return (
        strips[:, 0].reshape(128, columns.shape[1]),
        strips[:, 1].reshape(128, columns.shape[1]),
    )


def kernel(
    clips, cot, gain_in, shift_in, w_space, w_time,
    result_out, grad_out, taps_out,
    clips_v, cot4, w_space_v, w_time_v, w_space_t, w_time_t,
    hcat, mgcat, act_s, ng_s, h_t, h_tx, m_t, m_tx, mixed_own, mixed_halo, mixed_sib,
    stat_tx, stat_rx, mean_tx, mean_rx,
    rs_tx_a, rs_rx_a, rs_tx_b, rs_rx_b, z_tx, z_rx, fin_tx, gathered,
    gain, shift, result_v, grad_v, taps_v, local_sem, send_sem, recv_sem, piece_sem, known,
):
    clip = lax.axis_index("clip")
    frame = lax.axis_index("frame")
    xh, z = clip // ZS, lax.rem(clip, ZS)
    q, core = frame // 2, lax.rem(frame, 2)
    sibling = frame + 1 - 2 * core
    members = FRAMES * POS * (C // GROUPS)

    copies = [
        pltpu.make_async_copy(clips, clips_v, local_sem.at[0]),
        pltpu.make_async_copy(w_time, w_time_v, local_sem.at[1]),
        pltpu.make_async_copy(w_space, w_space_v, local_sem.at[2]),
        pltpu.make_async_copy(cot, cot4.at[core], local_sem.at[3]),
        pltpu.make_async_copy(gain_in, gain, local_sem.at[4]),
        pltpu.make_async_copy(shift_in, shift, local_sem.at[5]),
    ]
    for copy in copies:
        copy.start()

    barrier = pltpu.get_barrier_semaphore()

    def greet(clip_to, frame_to):
        pl.semaphore_signal(
            barrier, inc=1, device_id=(clip_to, frame_to), device_id_type=MESH
        )

    def greet_frame(i):
        greet(clip, lax.rem(frame + i + 1, FRAMES))

    def greet_plane(i):
        greet((1 - xh) * ZS + z, lax.rem(frame + 2 * i, FRAMES))

    def along(by):
        return xh * ZS + lax.rem(z + by + ZS, ZS)

    def tell(step):
        for by in (-(2**step), 2**step):
            pl.semaphore_signal(
                known.at[step], inc=1, device_id=(along(by), frame), device_id_type=MESH
            )

    loop(CHIPS, greet_plane)
    greet(along(-1), frame)
    greet(along(1), frame)
    loop(FRAMES - 1, greet_frame)

    zero = jnp.zeros((PAD, 3 * C), BF16)
    for buffer in (hcat, mgcat.at[0], mgcat.at[1]):
        buffer[0:PAD, :] = zero
        buffer[PAD + POS : PAD + POS + PAD, :] = zero

    copies[0].wait()
    values = clips_v[...].astype(F32)
    own_sum = group_spread(jnp.sum(values, axis=0, keepdims=True))
    own_mean = own_sum / (POS * (C // GROUPS))
    offset = values - own_mean
    own_squares = group_spread(jnp.sum(offset * offset, axis=0, keepdims=True))
    stat_tx[:, 0:C] = own_sum
    stat_tx[:, C : 2 * C] = own_squares
    copies[1].wait()
    for k in range(3):
        w_time_t[k] = w_time_v[k].T
    copies[4].wait()
    copies[5].wait()
    copies[2].wait()
    for p in range(3):
        for j in range(3):
            w_space_t[p, j * C : (j + 1) * C, :] = w_space_v[p, j * C : (j + 1) * C, :].T

    pl.semaphore_wait(barrier, CHIPS + 2 + FRAMES - 1)

    def share_stats(i):
        remote(
            stat_tx, stat_rx.at[i], send_sem.at[0], recv_sem.at[0],
            clip, lax.rem(frame + i + 1, FRAMES),
        ).start()

    loop(FRAMES - 1, share_stats)

    before = lax.rem(frame + FRAMES - 2, FRAMES)
    after = lax.rem(frame + 2, FRAMES)
    for n in range(CHUNKS):
        rows = pl.ds(n * PIECE, PIECE)
        remote(
            cot.at[rows], cot4.at[2 + core, rows], send_sem.at[1], piece_sem.at[n], clip, before
        ).start()
    remote(cot, cot4.at[core], send_sem.at[2], recv_sem.at[2], clip, sibling).start()

    tell(0)

    wait_for(stat_rx, recv_sem.at[0])
    own = stat_tx[...]
    sums = own[:, 0:C]
    squares = own[:, C : 2 * C]
    for i in range(FRAMES - 1):
        sums = sums + stat_rx[i, :, 0:C]
        squares = squares + stat_rx[i, :, C : 2 * C]
    center = sums / members
    part = POS * (C // GROUPS)
    away = own[:, 0:C] / part - center
    spread = away * away
    for i in range(FRAMES - 1):
        away = stat_rx[i, :, 0:C] / part - center
        spread = spread + away * away
    variance = (squares + part * spread) / members
    inv_std = lax.rsqrt(variance + EPSILON)

    column = lax.rem(lax.broadcasted_iota(jnp.int32, (POS, C), 0), COLS)
    normed = (clips_v[...].astype(F32) - center) * inv_std
    act = normed * gain[...] + shift[...]
    act_s[...] = act
    hidden = act / (1.0 + jnp.exp(-act))
    for j in range(3):
        hcat[PAD : PAD + POS, j * C : (j + 1) * C] = shifted(hidden, j - 1, column).astype(BF16)
    even, odd = by_parity(hidden.astype(BF16).T)
    first = core == 0
    h_tx[...] = jnp.where(first, odd, even)
    h_t[core] = jnp.where(first, even, odd)
    remote(h_tx, h_t.at[core], send_sem.at[3], recv_sem.at[3], clip, sibling).start()

    pl.semaphore_wait(known.at[0], 2)
    tell(1)

    for n in range(CHUNKS):
        rows = pl.ds(n * PIECE, PIECE)
        wait_for(cot4.at[2 + core, rows], piece_sem.at[n])
        remote(
            cot4.at[2 + core, rows], cot4.at[2 + core, rows],
            send_sem.at[4], recv_sem.at[4], clip, sibling,
        ).start()

    mixed = dot(hcat[0:POS, :], w_space_v[0])
    for p in range(1, 3):
        mixed = mixed + dot(hcat[p * COLS : p * COLS + POS, :], w_space_v[p])
    mixed = mixed.astype(BF16)
    mixed_own[...] = mixed
    even, odd = by_parity(mixed.T)
    m_tx[...] = jnp.where(first, odd, even)
    m_t[core] = jnp.where(first, even, odd)
    remote(m_tx, m_t.at[core], send_sem.at[5], recv_sem.at[5], clip, sibling).start()

    pl.semaphore_wait(known.at[1], 2)
    tell(2)

    copies[3].wait()
    wait_for(cot4.at[0], recv_sem.at[2])
    wait_for(cot4.at[0], recv_sem.at[4])
    wait_for(cot4.at[0], send_sem.at[4])

    @pl.when(q == CHIPS - 1)
    def _():
        cot4[2] = jnp.zeros((POS, C), BF16)
        cot4[3] = jnp.zeros((POS, C), BF16)

    for a in range(2):
        mg = dot(cot4[a], w_time_t[0]) + dot(cot4[a + 1], w_time_t[1])
        mg = mg + dot(cot4[a + 2], w_time_t[2])
        mg = mg.astype(BF16).astype(F32)
        for j in range(3):
            mgcat[a, PAD : PAD + POS, j * C : (j + 1) * C] = shifted(mg, 1 - j, column).astype(BF16)

    wait_for(h_t.at[0], recv_sem.at[3])
    for p in range(3):
        rows = pl.ds((2 - p) * COLS, POS)
        total = dot(h_t[0], mgcat[0, rows, :]) + dot(h_t[1], mgcat[1, rows, :])
        total = total.astype(BF16)
        for half in range(2):
            for to in range(CHIPS):
                for j in range(3):
                    rs_tx_a[half * CHIPS + to, 3 * p + j] = total[
                        to * 16 : to * 16 + 16, j * C + half * 128 : j * C + half * 128 + 128
                    ]

    def scatter(tx, rx, n):
        for i, (by_x, by_y) in enumerate(PLANE_ORDER):
            x = lax.rem(2 * xh + lax.rem(q, 2) + by_x, 2 * XH)
            y = lax.rem(q // 2 + by_y, CHIPS // 2)
            xh_to, q_to = x // 2, 2 * y + lax.rem(x, 2)
            remote(
                tx.at[xh_to * CHIPS + q_to], rx.at[i], send_sem.at[n], recv_sem.at[n],
                xh_to * ZS + z, 2 * q_to + core,
            ).start()

    scatter(rs_tx_a, rs_rx_a, 6)

    wait_for(m_t.at[0], recv_sem.at[5])
    for k in range(3):
        total = (dot(m_t[0], cot4[k]) + dot(m_t[1], cot4[k + 1])).astype(BF16)
        for half in range(2):
            for to in range(CHIPS):
                rs_tx_b[half * CHIPS + to, k] = total[
                    to * 16 : to * 16 + 16, half * 128 : half * 128 + 128
                ]

    scatter(rs_tx_b, rs_rx_b, 7)

    hidden_grad = dot(mgcat[core, 2 * COLS : 2 * COLS + POS, :], w_space_t[0])
    for p in range(1, 3):
        rows = pl.ds((2 - p) * COLS, POS)
        hidden_grad = hidden_grad + dot(mgcat[core, rows, :], w_space_t[p])
    act = act_s[...]
    s = 1.0 / (1.0 + jnp.exp(-act))
    ng = hidden_grad * s * (1.0 + act * (1.0 - s)) * gain[...]
    ng_s[...] = ng
    normed = (clips_v[...].astype(F32) - center) * inv_std
    mean_tx[:, 0:C] = group_spread(jnp.sum(ng, axis=0, keepdims=True))
    mean_tx[:, C : 2 * C] = group_spread(jnp.sum(ng * normed, axis=0, keepdims=True))

    def share_means(i):
        remote(
            mean_tx, mean_rx.at[i], send_sem.at[9], recv_sem.at[9],
            clip, lax.rem(frame + i + 1, FRAMES),
        ).start()

    loop(FRAMES - 1, share_means)

    me = xh * CHIPS + q

    def along_z(lowest, highest):
        def send(i):
            to = lax.rem(z + far_first(i), ZS)

            @pl.when((to >= lowest) & (to < highest))
            def _():
                remote(
                    z_tx.at[to], z_rx.at[ZS - 1 - far_first(i)],
                    send_sem.at[10], recv_sem.at[10], xh * ZS + to, frame,
                ).start()

        loop(ZS - 1, send)

    wait_for(rs_rx_a, recv_sem.at[6])
    for k in range(9):
        total = rs_tx_a[me, k].astype(F32)
        for i in range(XH * CHIPS - 1):
            total = total + rs_rx_a[i, k].astype(F32)
        z_tx[k] = total
    pl.semaphore_wait(known.at[2], 2)
    along_z(0, 9)
    wait_for(rs_rx_b, recv_sem.at[7])
    for k in range(3):
        total = rs_tx_b[me, k].astype(F32)
        for i in range(XH * CHIPS - 1):
            total = total + rs_rx_b[i, k].astype(F32)
        z_tx[9 + k] = total
    along_z(9, TAPS)

    remote(mixed_own, mixed_halo, send_sem.at[8], recv_sem.at[8], clip, after).start()

    wait_for(mean_rx, recv_sem.at[9])
    both = mean_tx[...]
    for i in range(FRAMES - 1):
        both = both + mean_rx[i]
    both = both / members
    m1, m2 = both[:, 0:C], both[:, C : 2 * C]
    normed = (clips_v[...].astype(F32) - center) * inv_std
    grad_v[...] = (
        cot4[core].astype(F32) + inv_std * (ng_s[...] - m1 - normed * m2)
    ).astype(BF16)
    grad_copy = pltpu.make_async_copy(grad_v, grad_out, local_sem.at[6])
    grad_copy.start()

    wait_for(mixed_halo, recv_sem.at[8])

    @pl.when(core == 0)
    def _():
        remote(mixed_own, mixed_sib, send_sem.at[11], recv_sem.at[11], clip, sibling).start()

    @pl.when(core == 1)
    def _():
        remote(mixed_halo, mixed_sib, send_sem.at[11], recv_sem.at[11], clip, sibling).start()

    temporal = dot(mixed_own[...], w_time_v[0])
    temporal = temporal + jnp.where(q > 0, dot(mixed_halo[...], w_time_v[2]), 0.0)
    wait_for(mixed_sib, recv_sem.at[11])
    temporal = temporal + jnp.where(frame > 0, dot(mixed_sib[...], w_time_v[1]), 0.0)
    result_v[...] = (clips_v[...].astype(F32) + temporal.astype(BF16).astype(F32)).astype(BF16)
    result_copy = pltpu.make_async_copy(result_v, result_out, local_sem.at[7])
    result_copy.start()

    scale = 1.0 / math.sqrt(XH * ZS * FRAMES * POS)

    @pl.when(z < TAPS)
    def _():
        wait_for(z_rx, recv_sem.at[10])
        total = z_tx[z]
        for i in range(ZS - 1):
            total = total + z_rx[i]
        done = (total * scale).astype(BF16)
        fin_tx[...] = done
        gathered[z * 2 + xh] = done

        def hand(clip_to):
            remote(
                fin_tx, gathered.at[z * 2 + xh], send_sem.at[12], recv_sem.at[12], clip_to, frame
            ).start()

        def hand_out(i):
            to = lax.rem(z + far_first(i), ZS)
            hand((1 - xh) * ZS + to)
            hand(xh * ZS + to)

        loop(ZS - 1, hand_out)
        hand((1 - xh) * ZS + z)
        wait_for(gathered.at[pl.ds(0, 2 * TAPS - 1)], recv_sem.at[12])
        wait_for(gathered.at[pl.ds(0, XH * ZS - 1)], send_sem.at[12])
        wait_for(z_tx.at[pl.ds(0, TAPS - 1)], send_sem.at[10])

    @pl.when(z >= TAPS)
    def _():
        wait_for(gathered.at[pl.ds(0, 2 * TAPS)], recv_sem.at[12])
        wait_for(z_tx, send_sem.at[10])

    for k in range(TAPS):
        for half in range(2):
            taps_v[k, :, half * 128 : half * 128 + 128] = gathered[2 * k + half]
    taps_copy = pltpu.make_async_copy(taps_v, taps_out, local_sem.at[8])
    taps_copy.start()

    wait_for(stat_rx, send_sem.at[0])
    wait_for(cot4.at[0], send_sem.at[1])
    wait_for(cot4.at[0], send_sem.at[2])
    wait_for(h_tx, send_sem.at[3])
    wait_for(m_tx, send_sem.at[5])
    wait_for(rs_rx_a, send_sem.at[6])
    wait_for(rs_rx_b, send_sem.at[7])
    wait_for(mixed_own, send_sem.at[8])
    wait_for(mean_rx, send_sem.at[9])
    wait_for(mixed_own, send_sem.at[11])
    for copy in (grad_copy, result_copy, taps_copy):
        copy.wait()


def write_out(result, grad, taps, result_out, grad_out, space_out, time_out, *scratch):
    result_v, grad_v, taps_v, in_sem, out_sem = scratch
    moves = [(taps, taps_v, ((0, 9, space_out), (9, 3, time_out)))]
    half = POS // 2
    for source, held, target in ((result, result_v, result_out), (grad, grad_v, grad_out)):
        for n in range(2):
            rows = pl.ds(n * half, half)
            moves.append((source.at[rows], held.at[rows], ((0, half, target.at[rows]),)))
    into = [
        pltpu.make_async_copy(source, held, in_sem.at[n])
        for n, (source, held, _) in enumerate(moves)
    ]
    for copy in into:
        copy.start()
    back = []
    for copy, (_, held, parts) in zip(into, moves):
        copy.wait()
        for first, count, target in parts:
            back.append(
                pltpu.make_async_copy(held.at[pl.ds(first, count)], target, out_sem.at[len(back)])
            )
            back[-1].start()
    for copy in back:
        copy.wait()


def per_device(clips, cotangent, norm_gain, norm_shift, w_spatial, w_time):
    hbm = pl.BlockSpec(memory_space=pltpu.HBM)
    blocks = pl.pallas_call(
        kernel,
        name="video_block",
        out_shape=(
            jax.ShapeDtypeStruct((POS, C), BF16),
            jax.ShapeDtypeStruct((POS, C), BF16),
            jax.ShapeDtypeStruct((TAPS, 16, C), BF16),
        ),
        in_specs=[hbm] * 6,
        out_specs=(hbm, hbm, hbm),
        scratch_shapes=[
            pltpu.VMEM((POS, C), BF16),
            pltpu.VMEM((4, POS, C), BF16),
            pltpu.VMEM((3, 3 * C, C), BF16),
            pltpu.VMEM((3, C, C), BF16),
            pltpu.VMEM((3, 3 * C, C), BF16),
            pltpu.VMEM((3, C, C), BF16),
            pltpu.VMEM((POS + 2 * PAD, 3 * C), BF16),
            pltpu.VMEM((2, POS + 2 * PAD, 3 * C), BF16),
            pltpu.VMEM((POS, C), F32),
            pltpu.VMEM((POS, C), F32),
            pltpu.VMEM((2, 128, POS), BF16),
            pltpu.VMEM((128, POS), BF16),
            pltpu.VMEM((2, 128, POS), BF16),
            pltpu.VMEM((128, POS), BF16),
            pltpu.VMEM((POS, C), BF16),
            pltpu.VMEM((POS, C), BF16),
            pltpu.VMEM((POS, C), BF16),
            pltpu.VMEM((1, 2 * C), F32),
            pltpu.VMEM((FRAMES - 1, 1, 2 * C), F32),
            pltpu.VMEM((1, 2 * C), F32),
            pltpu.VMEM((FRAMES - 1, 1, 2 * C), F32),
            pltpu.VMEM((XH * CHIPS, 9, 16, 128), BF16),
            pltpu.VMEM((XH * CHIPS - 1, 9, 16, 128), BF16),
            pltpu.VMEM((XH * CHIPS, 3, 16, 128), BF16),
            pltpu.VMEM((XH * CHIPS - 1, 3, 16, 128), BF16),
            pltpu.VMEM((TAPS, 16, 128), F32),
            pltpu.VMEM((ZS - 1, 16, 128), F32),
            pltpu.VMEM((16, 128), BF16),
            pltpu.VMEM((XH * ZS - 1, 16, 128), BF16),
            pltpu.VMEM((1, C), F32),
            pltpu.VMEM((1, C), F32),
            pltpu.VMEM((POS, C), BF16),
            pltpu.VMEM((POS, C), BF16),
            pltpu.VMEM((TAPS, 16, C), BF16),
            pltpu.SemaphoreType.DMA((9,)),
            pltpu.SemaphoreType.DMA((13,)),
            pltpu.SemaphoreType.DMA((13,)),
            pltpu.SemaphoreType.DMA((CHUNKS,)),
            pltpu.SemaphoreType.REGULAR((3,)),
        ],
        compiler_params=pltpu.CompilerParams(
            collective_id=0, has_side_effects=True, vmem_limit_bytes=VMEM_BYTES
        ),
    )(
        clips.reshape(POS, C),
        cotangent.reshape(POS, C),
        norm_gain.reshape(1, C),
        norm_shift.reshape(1, C),
        w_spatial.reshape(3, 3 * C, C),
        w_time,
    )
    result, grad, space, time = pl.pallas_call(
        write_out,
        name="write_out",
        out_shape=(
            jax.ShapeDtypeStruct((POS, C), BF16),
            jax.ShapeDtypeStruct((POS, C), BF16),
            jax.ShapeDtypeStruct((9, 16, C), BF16),
            jax.ShapeDtypeStruct((3, 16, C), BF16),
        ),
        in_specs=[hbm, hbm, hbm],
        out_specs=(hbm, hbm, hbm, hbm),
        scratch_shapes=[
            pltpu.VMEM((POS, C), BF16),
            pltpu.VMEM((POS, C), BF16),
            pltpu.VMEM((TAPS, 16, C), BF16),
            pltpu.SemaphoreType.DMA((5,)),
            pltpu.SemaphoreType.DMA((6,)),
        ],
        compiler_params=pltpu.CompilerParams(vmem_limit_bytes=VMEM_BYTES),
    )(*blocks)
    return (
        result.reshape(clips.shape),
        grad.reshape(clips.shape),
        space.reshape(3, 3, 16, C),
        time,
    )


def solution(mesh):
    placed = (
        P("clip", "frame", None, None, None),
        P("clip", "frame", None, None, None),
        P(),
        P(),
        P(),
        P(),
    )
    return jax.shard_map(
        per_device,
        mesh=mesh,
        in_specs=placed,
        out_specs=(
            P("clip", "frame", None, None, None),
            P("clip", "frame", None, None, None),
            P(None, None, "frame", None),
            P(None, "frame", None),
        ),
        check_vma=False,
    )
```

```python
import functools
import math

import jax
import jax.numpy as jnp
from jax import lax
from jax.experimental import pallas as pl
from jax.experimental.pallas import tpu as pltpu
from jax.sharding import PartitionSpec as P

GROUPS = 32
EPSILON = 1e-05
MESH = pl.DeviceIdType.MESH
F32 = jnp.float32
BF16 = jnp.bfloat16

ROWS, COLS, C = 16, 32, 256
POS = ROWS * COLS
PAD = COLS
TAPS = 12
VMEM_BYTES = 60 * 2**20

FRAME_ORDER = (
    (2, 1, 0), (2, 1, 1), (2, 0, 0), (2, 0, 1), (1, 1, 0), (1, 1, 1), (3, 1, 0), (3, 1, 1),
    (1, 0, 0), (1, 0, 1), (3, 0, 0), (3, 0, 1), (0, 1, 0), (0, 1, 1), (0, 0, 1),
)

PLANE_ORDER = (
    (2, 2), (1, 0), (0, 1), (2, 1), (0, 3), (3, 0), (1, 2), (1, 1),
    (2, 3), (3, 3), (3, 2), (0, 2), (2, 0), (3, 1), (1, 3),
)
CHUNKS = 4
PIECE = POS // CHUNKS

ZS, XH, CHIPS = 16, 2, 8
FRAMES = 2 * CHIPS


def dot(a, b):
    return jnp.dot(a, b, preferred_element_type=F32)


def remote(src, dst, send_sem, recv_sem, clip, frame):
    return pltpu.make_async_remote_copy(
        src_ref=src,
        dst_ref=dst,
        send_sem=send_sem,
        recv_sem=recv_sem,
        device_id=(clip, frame),
        device_id_type=MESH,
    )


def wait_for(ref, sem):
    pltpu.make_async_copy(ref, ref, sem).wait()


def loop(count, body):
    def step(i, carry):
        body(i)
        return carry

    lax.fori_loop(0, count, step, 0)


def far_first(i):
    return ZS // 2 + ((i + 1) // 2) * (1 - 2 * lax.rem(i, 2))


def group_spread(row):
    lane = lax.broadcasted_iota(jnp.int32, row.shape, 1)
    for bit in (1, 2, 4):
        up = pltpu.roll(row, bit, 1)
        down = pltpu.roll(row, row.shape[1] - bit, 1)
        row = row + jnp.where((lane & bit) != 0, up, down)
    return row


def shifted(values, by, column):
    if by == 0:
        return values
    rolled = pltpu.roll(values, (-by) % values.shape[0], 0)
    edge = 0 if by < 0 else COLS - 1
    return jnp.where(column == edge, 0.0, rolled)


def by_parity(columns):
    strips = columns.reshape(8, 2, 16, columns.shape[1])
    return (
        strips[:, 0].reshape(128, columns.shape[1]),
        strips[:, 1].reshape(128, columns.shape[1]),
    )


def kernel(
    clips, cot, gain_in, shift_in, w_space, w_time,
    result_out, grad_out, taps_out,
    clips_v, cot4, w_space_v, w_time_v, w_space_t, w_time_t,
    hcat, mgcat, act_s, hid_s, hid_grad_s, ng_s, h_t, h_tx, m_t, m_tx, mixed_own, mixed_halo, mixed_sib,
    stat_tx, stat_rx, mean_tx, mean_rx,
    rs_tx_a, rs_rx_a, rs_tx_b, rs_rx_b, z_tx, z_rx, fin_tx, gathered,
    gain, shift, result_v, grad_v, taps_v, local_sem, send_sem, recv_sem, piece_sem, known,
):
    clip = lax.axis_index("clip")
    frame = lax.axis_index("frame")
    xh, z = clip // ZS, lax.rem(clip, ZS)
    q, core = frame // 2, lax.rem(frame, 2)
    sibling = frame + 1 - 2 * core
    members = FRAMES * POS * (C // GROUPS)

    barrier = pltpu.get_barrier_semaphore()

    def greet(clip_to, frame_to):
        pl.semaphore_signal(
            barrier, inc=1, device_id=(clip_to, frame_to), device_id_type=MESH
        )

    def along(by):
        return xh * ZS + lax.rem(z + by + ZS, ZS)

    def tell(step):
        for by in (-(2**step), 2**step):
            pl.semaphore_signal(
                known.at[step], inc=1, device_id=(along(by), frame), device_id_type=MESH
            )

    y, x_lo = q // 2, lax.rem(q, 2)
    other = (1 - xh) * ZS + z
    mates = [
        4 * lax.rem(y + by_y, CHIPS // 2)
        + 2 * (1 - x_lo if by_x else x_lo)
        + (1 - core if by_core else core)
        for by_y, by_x, by_core in FRAME_ORDER
    ]
    for mate in mates:
        greet(clip, mate)
    greet(other, frame)
    greet(along(-1), frame)
    greet(along(1), frame)

    copies = [
        pltpu.make_async_copy(clips, clips_v, local_sem.at[0]),
        pltpu.make_async_copy(w_time, w_time_v, local_sem.at[1]),
        pltpu.make_async_copy(w_space, w_space_v, local_sem.at[2]),
        pltpu.make_async_copy(cot, cot4.at[core], local_sem.at[3]),
        pltpu.make_async_copy(gain_in, gain, local_sem.at[4]),
        pltpu.make_async_copy(shift_in, shift, local_sem.at[5]),
    ]
    for copy in copies:
        copy.start()

    zero = jnp.zeros((PAD, 3 * C), BF16)
    for buffer in (hcat, mgcat.at[0], mgcat.at[1]):
        buffer[0:PAD, :] = zero
        buffer[PAD + POS : PAD + POS + PAD, :] = zero

    copies[0].wait()
    values = clips_v[...].astype(F32)
    own_sum = group_spread(jnp.sum(values, axis=0, keepdims=True))
    own_mean = own_sum / (POS * (C // GROUPS))
    offset = values - own_mean
    own_squares = group_spread(jnp.sum(offset * offset, axis=0, keepdims=True))
    stat_tx[:, 0:C] = own_sum
    stat_tx[:, C : 2 * C] = own_squares
    pl.semaphore_wait(barrier, FRAMES - 1 + 3)

    for i, mate in enumerate(mates):
        remote(stat_tx, stat_rx.at[i], send_sem.at[0], recv_sem.at[0], clip, mate).start()

    before = lax.rem(frame + FRAMES - 2, FRAMES)
    after = lax.rem(frame + 2, FRAMES)
    for n in range(CHUNKS):
        rows = pl.ds(n * PIECE, PIECE)
        remote(
            cot.at[rows], cot4.at[2 + core, rows], send_sem.at[1], piece_sem.at[n], clip, before
        ).start()
    remote(cot, cot4.at[core], send_sem.at[2], recv_sem.at[2], clip, sibling).start()

    tell(0)
    pl.semaphore_signal(known.at[3], inc=1, device_id=(other, frame), device_id_type=MESH)

    copies[1].wait()
    for k in range(3):
        w_time_t[k] = w_time_v[k].T
    copies[4].wait()
    copies[5].wait()
    copies[2].wait()
    for p in range(3):
        for j in range(3):
            w_space_t[p, j * C : (j + 1) * C, :] = w_space_v[p, j * C : (j + 1) * C, :].T

    wait_for(stat_rx, recv_sem.at[0])
    own = stat_tx[...]
    sums = own[:, 0:C]
    squares = own[:, C : 2 * C]
    for i in range(FRAMES - 1):
        sums = sums + stat_rx[i, :, 0:C]
        squares = squares + stat_rx[i, :, C : 2 * C]
    center = sums / members
    part = POS * (C // GROUPS)
    away = own[:, 0:C] / part - center
    spread = away * away
    for i in range(FRAMES - 1):
        away = stat_rx[i, :, 0:C] / part - center
        spread = spread + away * away
    variance = (squares + part * spread) / members
    inv_std = lax.rsqrt(variance + EPSILON)

    column = lax.rem(lax.broadcasted_iota(jnp.int32, (POS, C), 0), COLS)
    normed = (clips_v[...].astype(F32) - center) * inv_std
    act = normed * gain[...] + shift[...]
    act_s[...] = act
    hidden = act / (1.0 + jnp.exp(-act))
    hid_s[...] = hidden
    even, odd = by_parity(hidden.astype(BF16).T)
    first = core == 0
    h_tx[...] = jnp.where(first, odd, even)
    h_t[core] = jnp.where(first, even, odd)
    remote(h_tx, h_t.at[core], send_sem.at[3], recv_sem.at[3], clip, sibling).start()

    for n in range(CHUNKS):
        rows = pl.ds(n * PIECE, PIECE)
        wait_for(cot4.at[2 + core, rows], piece_sem.at[n])
        remote(
            cot4.at[2 + core, rows], cot4.at[2 + core, rows],
            send_sem.at[4], recv_sem.at[4], clip, sibling,
        ).start()

    copies[3].wait()
    wait_for(cot4.at[0], recv_sem.at[2])
    ng_s[...] = dot(cot4[0], w_time_t[0]) + dot(cot4[1], w_time_t[1])
    hid_grad_s[...] = dot(cot4[1], w_time_t[0])
    wait_for(cot4.at[0], recv_sem.at[4])
    wait_for(cot4.at[0], send_sem.at[4])

    @pl.when(q == CHIPS - 1)
    def _():
        cot4[2] = jnp.zeros((POS, C), BF16)
        cot4[3] = jnp.zeros((POS, C), BF16)

    for a in range(2):
        if a == 0:
            mg = ng_s[...] + dot(cot4[2], w_time_t[2])
        else:
            mg = hid_grad_s[...] + dot(cot4[2], w_time_t[1]) + dot(cot4[3], w_time_t[2])
        mg = mg.astype(BF16).astype(F32)
        for j in range(3):
            mgcat[a, PAD : PAD + POS, j * C : (j + 1) * C] = shifted(mg, 1 - j, column).astype(BF16)

    pl.semaphore_wait(known.at[0], 2)
    tell(1)

    wait_for(h_t.at[0], recv_sem.at[3])
    for p in range(3):
        rows = pl.ds((2 - p) * COLS, POS)
        total = dot(h_t[0], mgcat[0, rows, :]) + dot(h_t[1], mgcat[1, rows, :])
        total = total.astype(BF16)
        for half in range(2):
            for to in range(CHIPS):
                for j in range(3):
                    rs_tx_a[half * CHIPS + to, 3 * p + j] = total[
                        to * 16 : to * 16 + 16, j * C + half * 128 : j * C + half * 128 + 128
                    ]

    def scatter(tx, rx, n):
        for i, (by_x, by_y) in enumerate(PLANE_ORDER):
            x = lax.rem(2 * xh + lax.rem(q, 2) + by_x, 2 * XH)
            y = lax.rem(q // 2 + by_y, CHIPS // 2)
            xh_to, q_to = x // 2, 2 * y + lax.rem(x, 2)
            remote(
                tx.at[xh_to * CHIPS + q_to], rx.at[i], send_sem.at[n], recv_sem.at[n],
                xh_to * ZS + z, 2 * q_to + core,
            ).start()

    pl.semaphore_wait(known.at[3], 1)
    scatter(rs_tx_a, rs_rx_a, 6)

    hidden = hid_s[...]
    for j in range(3):
        hcat[PAD : PAD + POS, j * C : (j + 1) * C] = shifted(hidden, j - 1, column).astype(BF16)
    mixed = dot(hcat[0:POS, :], w_space_v[0])
    for p in range(1, 3):
        mixed = mixed + dot(hcat[p * COLS : p * COLS + POS, :], w_space_v[p])
    mixed = mixed.astype(BF16)
    mixed_own[...] = mixed
    even, odd = by_parity(mixed.T)
    m_tx[...] = jnp.where(first, odd, even)
    m_t[core] = jnp.where(first, even, odd)
    remote(m_tx, m_t.at[core], send_sem.at[5], recv_sem.at[5], clip, sibling).start()

    wait_for(m_t.at[0], recv_sem.at[5])
    for k in range(3):
        total = (dot(m_t[0], cot4[k]) + dot(m_t[1], cot4[k + 1])).astype(BF16)
        for half in range(2):
            for to in range(CHIPS):
                rs_tx_b[half * CHIPS + to, k] = total[
                    to * 16 : to * 16 + 16, half * 128 : half * 128 + 128
                ]

    scatter(rs_tx_b, rs_rx_b, 7)
    pl.semaphore_wait(known.at[1], 2)
    tell(2)

    hidden_grad = dot(mgcat[core, 2 * COLS : 2 * COLS + POS, :], w_space_t[0])
    for p in range(1, 3):
        rows = pl.ds((2 - p) * COLS, POS)
        hidden_grad = hidden_grad + dot(mgcat[core, rows, :], w_space_t[p])
    act = act_s[...]
    s = 1.0 / (1.0 + jnp.exp(-act))
    ng = hidden_grad * s * (1.0 + act * (1.0 - s)) * gain[...]
    ng_s[...] = ng
    normed = (clips_v[...].astype(F32) - center) * inv_std
    mean_tx[:, 0:C] = group_spread(jnp.sum(ng, axis=0, keepdims=True))
    mean_tx[:, C : 2 * C] = group_spread(jnp.sum(ng * normed, axis=0, keepdims=True))

    for i, mate in enumerate(mates):
        remote(mean_tx, mean_rx.at[i], send_sem.at[9], recv_sem.at[9], clip, mate).start()

    me = xh * CHIPS + q

    def along_z(lowest, highest):
        def send(i):
            to = lax.rem(z + far_first(i), ZS)

            tap = to - to // 4

            @pl.when((lax.rem(to, 4) < 3) & (tap >= lowest) & (tap < highest))
            def _():
                remote(
                    z_tx.at[tap], z_rx.at[ZS - 1 - far_first(i)],
                    send_sem.at[10], recv_sem.at[10], xh * ZS + to, frame,
                ).start()

        loop(ZS - 1, send)

    wait_for(rs_rx_a, recv_sem.at[6])
    for k in range(9):
        total = rs_tx_a[me, k].astype(F32)
        for i in range(XH * CHIPS - 1):
            total = total + rs_rx_a[i, k].astype(F32)
        z_tx[k] = total
    pl.semaphore_wait(known.at[2], 2)
    along_z(0, 9)
    wait_for(rs_rx_b, recv_sem.at[7])
    for k in range(3):
        total = rs_tx_b[me, k].astype(F32)
        for i in range(XH * CHIPS - 1):
            total = total + rs_rx_b[i, k].astype(F32)
        z_tx[9 + k] = total
    along_z(9, TAPS)

    remote(mixed_own, mixed_halo, send_sem.at[8], recv_sem.at[8], clip, after).start()

    wait_for(mean_rx, recv_sem.at[9])
    both = mean_tx[...]
    for i in range(FRAMES - 1):
        both = both + mean_rx[i]
    both = both / members
    m1, m2 = both[:, 0:C], both[:, C : 2 * C]
    normed = (clips_v[...].astype(F32) - center) * inv_std
    grad_v[...] = (
        cot4[core].astype(F32) + inv_std * (ng_s[...] - m1 - normed * m2)
    ).astype(BF16)
    grad_copy = pltpu.make_async_copy(grad_v, grad_out, local_sem.at[6])
    grad_copy.start()

    scale = 1.0 / math.sqrt(XH * ZS * FRAMES * POS)

    @pl.when(lax.rem(z, 4) < 3)
    def _():
        wait_for(z_rx, recv_sem.at[10])
        tap = z - z // 4
        total = z_tx[tap]
        for i in range(ZS - 1):
            total = total + z_rx[i]
        done = (total * scale).astype(BF16)
        fin_tx[...] = done
        gathered[tap * 2 + xh] = done

        def hand(clip_to):
            remote(
                fin_tx, gathered.at[tap * 2 + xh], send_sem.at[12], recv_sem.at[12], clip_to, frame
            ).start()

        def hand_out(i):
            to = lax.rem(z + far_first(i), ZS)
            hand((1 - xh) * ZS + to)
            hand(xh * ZS + to)

        loop(ZS - 1, hand_out)
        hand((1 - xh) * ZS + z)

    wait_for(mixed_halo, recv_sem.at[8])

    @pl.when(core == 0)
    def _():
        remote(mixed_own, mixed_sib, send_sem.at[11], recv_sem.at[11], clip, sibling).start()

    @pl.when(core == 1)
    def _():
        remote(mixed_halo, mixed_sib, send_sem.at[11], recv_sem.at[11], clip, sibling).start()

    temporal = dot(mixed_own[...], w_time_v[0])
    temporal = temporal + jnp.where(q > 0, dot(mixed_halo[...], w_time_v[2]), 0.0)
    wait_for(mixed_sib, recv_sem.at[11])
    temporal = temporal + jnp.where(frame > 0, dot(mixed_sib[...], w_time_v[1]), 0.0)
    result_v[...] = (clips_v[...].astype(F32) + temporal.astype(BF16).astype(F32)).astype(BF16)
    result_copy = pltpu.make_async_copy(result_v, result_out, local_sem.at[7])
    result_copy.start()

    @pl.when(lax.rem(z, 4) < 3)
    def _():
        wait_for(gathered.at[pl.ds(0, 2 * TAPS - 1)], recv_sem.at[12])
        wait_for(gathered.at[pl.ds(0, XH * ZS - 1)], send_sem.at[12])
        wait_for(z_tx.at[pl.ds(0, TAPS - 1)], send_sem.at[10])

    @pl.when(lax.rem(z, 4) == 3)
    def _():
        wait_for(gathered.at[pl.ds(0, 2 * TAPS)], recv_sem.at[12])
        wait_for(z_tx, send_sem.at[10])

    for k in range(TAPS):
        for half in range(2):
            taps_v[k, :, half * 128 : half * 128 + 128] = gathered[2 * k + half]
    taps_copy = pltpu.make_async_copy(taps_v, taps_out, local_sem.at[8])
    taps_copy.start()

    wait_for(stat_rx, send_sem.at[0])
    wait_for(cot4.at[0], send_sem.at[1])
    wait_for(cot4.at[0], send_sem.at[2])
    wait_for(h_tx, send_sem.at[3])
    wait_for(m_tx, send_sem.at[5])
    wait_for(rs_rx_a, send_sem.at[6])
    wait_for(rs_rx_b, send_sem.at[7])
    wait_for(mixed_own, send_sem.at[8])
    wait_for(mean_rx, send_sem.at[9])
    wait_for(mixed_own, send_sem.at[11])
    for copy in (grad_copy, result_copy, taps_copy):
        copy.wait()


def write_out(result, grad, taps, result_out, grad_out, space_out, time_out, *scratch):
    result_v, grad_v, taps_v, in_sem, out_sem = scratch
    moves = [(taps, taps_v, ((0, 9, space_out), (9, 3, time_out)))]
    half = POS // 2
    for source, held, target in ((result, result_v, result_out), (grad, grad_v, grad_out)):
        for n in range(2):
            rows = pl.ds(n * half, half)
            moves.append((source.at[rows], held.at[rows], ((0, half, target.at[rows]),)))
    into = [
        pltpu.make_async_copy(source, held, in_sem.at[n])
        for n, (source, held, _) in enumerate(moves)
    ]
    for copy in into:
        copy.start()
    back = []
    for copy, (_, held, parts) in zip(into, moves):
        copy.wait()
        for first, count, target in parts:
            back.append(
                pltpu.make_async_copy(held.at[pl.ds(first, count)], target, out_sem.at[len(back)])
            )
            back[-1].start()
    for copy in back:
        copy.wait()


def per_device(clips, cotangent, norm_gain, norm_shift, w_spatial, w_time):
    hbm = pl.BlockSpec(memory_space=pltpu.HBM)
    blocks = pl.pallas_call(
        kernel,
        name="video_block",
        out_shape=(
            jax.ShapeDtypeStruct((POS, C), BF16),
            jax.ShapeDtypeStruct((POS, C), BF16),
            jax.ShapeDtypeStruct((TAPS, 16, C), BF16),
        ),
        in_specs=[hbm] * 6,
        out_specs=(hbm, hbm, hbm),
        scratch_shapes=[
            pltpu.VMEM((POS, C), BF16),
            pltpu.VMEM((4, POS, C), BF16),
            pltpu.VMEM((3, 3 * C, C), BF16),
            pltpu.VMEM((3, C, C), BF16),
            pltpu.VMEM((3, 3 * C, C), BF16),
            pltpu.VMEM((3, C, C), BF16),
            pltpu.VMEM((POS + 2 * PAD, 3 * C), BF16),
            pltpu.VMEM((2, POS + 2 * PAD, 3 * C), BF16),
            pltpu.VMEM((POS, C), F32),
            pltpu.VMEM((POS, C), F32),
            pltpu.VMEM((POS, C), F32),
            pltpu.VMEM((POS, C), F32),
            pltpu.VMEM((2, 128, POS), BF16),
            pltpu.VMEM((128, POS), BF16),
            pltpu.VMEM((2, 128, POS), BF16),
            pltpu.VMEM((128, POS), BF16),
            pltpu.VMEM((POS, C), BF16),
            pltpu.VMEM((POS, C), BF16),
            pltpu.VMEM((POS, C), BF16),
            pltpu.VMEM((1, 2 * C), F32),
            pltpu.VMEM((FRAMES - 1, 1, 2 * C), F32),
            pltpu.VMEM((1, 2 * C), F32),
            pltpu.VMEM((FRAMES - 1, 1, 2 * C), F32),
            pltpu.VMEM((XH * CHIPS, 9, 16, 128), BF16),
            pltpu.VMEM((XH * CHIPS - 1, 9, 16, 128), BF16),
            pltpu.VMEM((XH * CHIPS, 3, 16, 128), BF16),
            pltpu.VMEM((XH * CHIPS - 1, 3, 16, 128), BF16),
            pltpu.VMEM((TAPS, 16, 128), F32),
            pltpu.VMEM((ZS - 1, 16, 128), F32),
            pltpu.VMEM((16, 128), BF16),
            pltpu.VMEM((XH * ZS - 1, 16, 128), BF16),
            pltpu.VMEM((1, C), F32),
            pltpu.VMEM((1, C), F32),
            pltpu.VMEM((POS, C), BF16),
            pltpu.VMEM((POS, C), BF16),
            pltpu.VMEM((TAPS, 16, C), BF16),
            pltpu.SemaphoreType.DMA((9,)),
            pltpu.SemaphoreType.DMA((13,)),
            pltpu.SemaphoreType.DMA((13,)),
            pltpu.SemaphoreType.DMA((CHUNKS,)),
            pltpu.SemaphoreType.REGULAR((4,)),
        ],
        compiler_params=pltpu.CompilerParams(
            collective_id=0, has_side_effects=True, vmem_limit_bytes=VMEM_BYTES
        ),
    )(
        clips.reshape(POS, C),
        cotangent.reshape(POS, C),
        norm_gain.reshape(1, C),
        norm_shift.reshape(1, C),
        w_spatial.reshape(3, 3 * C, C),
        w_time,
    )
    result, grad, space, time = pl.pallas_call(
        write_out,
        name="write_out",
        out_shape=(
            jax.ShapeDtypeStruct((POS, C), BF16),
            jax.ShapeDtypeStruct((POS, C), BF16),
            jax.ShapeDtypeStruct((9, 16, C), BF16),
            jax.ShapeDtypeStruct((3, 16, C), BF16),
        ),
        in_specs=[hbm, hbm, hbm],
        out_specs=(hbm, hbm, hbm, hbm),
        scratch_shapes=[
            pltpu.VMEM((POS, C), BF16),
            pltpu.VMEM((POS, C), BF16),
            pltpu.VMEM((TAPS, 16, C), BF16),
            pltpu.SemaphoreType.DMA((5,)),
            pltpu.SemaphoreType.DMA((6,)),
        ],
        compiler_params=pltpu.CompilerParams(vmem_limit_bytes=VMEM_BYTES),
    )(*blocks)
    return (
        result.reshape(clips.shape),
        grad.reshape(clips.shape),
        space.reshape(3, 3, 16, C),
        time,
    )


def solution(mesh):
    placed = (
        P("clip", "frame", None, None, None),
        P("clip", "frame", None, None, None),
        P(),
        P(),
        P(),
        P(),
    )
    return jax.shard_map(
        per_device,
        mesh=mesh,
        in_specs=placed,
        out_specs=(
            P("clip", "frame", None, None, None),
            P("clip", "frame", None, None, None),
            P(None, None, "frame", None),
            P(None, "frame", None),
        ),
        check_vma=False,
    )
```

```python
import functools
import math

import jax
import jax.numpy as jnp
from jax import lax
from jax.experimental import pallas as pl
from jax.experimental.pallas import tpu as pltpu
from jax.sharding import PartitionSpec as P

GROUPS = 32
EPSILON = 1e-05
MESH = pl.DeviceIdType.MESH
F32 = jnp.float32
BF16 = jnp.bfloat16

ROWS, COLS, C = 16, 32, 256
POS = ROWS * COLS
PAD = COLS
TAPS = 12
VMEM_BYTES = 60 * 2**20

FRAME_ORDER = (
    (2, 1, 0), (2, 1, 1), (2, 0, 0), (2, 0, 1), (1, 1, 0), (1, 1, 1), (3, 1, 0), (3, 1, 1),
    (1, 0, 0), (1, 0, 1), (3, 0, 0), (3, 0, 1), (0, 1, 0), (0, 1, 1), (0, 0, 1),
)

PLANE_ORDER = (
    (2, 2), (2, 1), (1, 2), (2, 3), (3, 2), (1, 1), (3, 3), (1, 3),
    (3, 1), (2, 0), (0, 2), (1, 0), (0, 1), (3, 0), (0, 3),
)
CHUNKS = 4
PIECE = POS // CHUNKS

ZS, XH, CHIPS = 16, 2, 8
HALF = ZS // 2
FRAMES = 2 * CHIPS


def dot(a, b):
    return jnp.dot(a, b, preferred_element_type=F32)


def remote(src, dst, send_sem, recv_sem, clip, frame):
    return pltpu.make_async_remote_copy(
        src_ref=src,
        dst_ref=dst,
        send_sem=send_sem,
        recv_sem=recv_sem,
        device_id=(clip, frame),
        device_id_type=MESH,
    )


def wait_for(ref, sem):
    pltpu.make_async_copy(ref, ref, sem).wait()


def loop(count, body):
    def step(i, carry):
        body(i)
        return carry

    lax.fori_loop(0, count, step, 0)


def group_spread(row):
    lane = lax.broadcasted_iota(jnp.int32, row.shape, 1)
    for bit in (1, 2, 4):
        up = pltpu.roll(row, bit, 1)
        down = pltpu.roll(row, row.shape[1] - bit, 1)
        row = row + jnp.where((lane & bit) != 0, up, down)
    return row


def shifted(values, by, column):
    if by == 0:
        return values
    rolled = pltpu.roll(values, (-by) % values.shape[0], 0)
    edge = 0 if by < 0 else COLS - 1
    return jnp.where(column == edge, 0.0, rolled)


def by_parity(columns):
    strips = columns.reshape(8, 2, 16, columns.shape[1])
    return (
        strips[:, 0].reshape(128, columns.shape[1]),
        strips[:, 1].reshape(128, columns.shape[1]),
    )


def kernel(
    clips, cot, gain_in, shift_in, w_space, w_time,
    result_out, grad_out, taps_out,
    clips_v, cot4, w_space_v, w_time_v, w_space_t, w_time_t,
    hcat, mgcat, act_s, hid_grad_s, ng_s, h_t, h_tx, m_t, m_tx, mixed_own, mixed_halo, mixed_sib,
    stat_tx, stat_rx, mean_tx, mean_rx,
    rs_tx_a, rs_rx_a, rs_tx_b, rs_rx_b, rs_tx_c, rs_rx_c, z_tx, z_rx, fin_tx, gathered,
    gain, shift, result_v, grad_v, taps_v, local_sem, send_sem, recv_sem, piece_sem, known,
):
    clip = lax.axis_index("clip")
    frame = lax.axis_index("frame")
    xh, z = clip // ZS, lax.rem(clip, ZS)
    q, core = frame // 2, lax.rem(frame, 2)
    sibling = frame + 1 - 2 * core
    members = FRAMES * POS * (C // GROUPS)

    barrier = pltpu.get_barrier_semaphore()

    def greet(clip_to, frame_to):
        pl.semaphore_signal(
            barrier, inc=1, device_id=(clip_to, frame_to), device_id_type=MESH
        )

    def along(by):
        return xh * ZS + lax.rem(z + by + ZS, ZS)

    def tell(step):
        for by in (-(2**step), 2**step):
            pl.semaphore_signal(
                known.at[step], inc=1, device_id=(along(by), frame), device_id_type=MESH
            )

    y, x_lo = q // 2, lax.rem(q, 2)
    other = (1 - xh) * ZS + z
    mates = [
        4 * lax.rem(y + by_y, CHIPS // 2)
        + 2 * (1 - x_lo if by_x else x_lo)
        + (1 - core if by_core else core)
        for by_y, by_x, by_core in FRAME_ORDER
    ]
    for mate in mates:
        greet(clip, mate)
    greet(other, frame)
    greet(along(-1), frame)
    greet(along(1), frame)

    copies = [
        pltpu.make_async_copy(clips, clips_v, local_sem.at[0]),
        pltpu.make_async_copy(w_time, w_time_v, local_sem.at[1]),
        pltpu.make_async_copy(w_space, w_space_v, local_sem.at[2]),
        pltpu.make_async_copy(cot, cot4.at[core], local_sem.at[3]),
        pltpu.make_async_copy(gain_in, gain, local_sem.at[4]),
        pltpu.make_async_copy(shift_in, shift, local_sem.at[5]),
    ]
    for copy in copies:
        copy.start()

    zero = jnp.zeros((PAD, 3 * C), BF16)
    for buffer in (hcat, mgcat.at[0], mgcat.at[1]):
        buffer[0:PAD, :] = zero
        buffer[PAD + POS : PAD + POS + PAD, :] = zero

    copies[0].wait()
    values = clips_v[...].astype(F32)
    own_sum = group_spread(jnp.sum(values, axis=0, keepdims=True))
    own_mean = own_sum / (POS * (C // GROUPS))
    offset = values - own_mean
    own_squares = group_spread(jnp.sum(offset * offset, axis=0, keepdims=True))
    stat_tx[:, 0:C] = own_sum
    stat_tx[:, C : 2 * C] = own_squares
    pl.semaphore_wait(barrier, FRAMES - 1 + 3)

    for i, mate in enumerate(mates):
        remote(stat_tx, stat_rx.at[i], send_sem.at[0], recv_sem.at[0], clip, mate).start()

    before = lax.rem(frame + FRAMES - 2, FRAMES)
    after = lax.rem(frame + 2, FRAMES)
    for n in range(CHUNKS):
        rows = pl.ds(n * PIECE, PIECE)
        remote(
            cot.at[rows], cot4.at[2 + core, rows], send_sem.at[1], piece_sem.at[n], clip, before
        ).start()
    remote(cot, cot4.at[core], send_sem.at[2], recv_sem.at[2], clip, sibling).start()

    tell(0)
    pl.semaphore_signal(known.at[3], inc=1, device_id=(other, frame), device_id_type=MESH)

    copies[1].wait()
    for k in range(3):
        w_time_t[k] = w_time_v[k].T
    copies[4].wait()
    copies[5].wait()
    copies[2].wait()
    for p in range(3):
        for j in range(3):
            w_space_t[p, j * C : (j + 1) * C, :] = w_space_v[p, j * C : (j + 1) * C, :].T

    wait_for(stat_rx, recv_sem.at[0])
    own = stat_tx[...]
    sums = own[:, 0:C]
    squares = own[:, C : 2 * C]
    for i in range(FRAMES - 1):
        sums = sums + stat_rx[i, :, 0:C]
        squares = squares + stat_rx[i, :, C : 2 * C]
    center = sums / members
    part = POS * (C // GROUPS)
    away = own[:, 0:C] / part - center
    spread = away * away
    for i in range(FRAMES - 1):
        away = stat_rx[i, :, 0:C] / part - center
        spread = spread + away * away
    variance = (squares + part * spread) / members
    inv_std = lax.rsqrt(variance + EPSILON)

    column = lax.rem(lax.broadcasted_iota(jnp.int32, (POS, C), 0), COLS)
    normed = (clips_v[...].astype(F32) - center) * inv_std
    act = normed * gain[...] + shift[...]
    act_s[...] = act
    hidden = act / (1.0 + jnp.exp(-act))
    even, odd = by_parity(hidden.astype(BF16).T)
    first = core == 0
    h_tx[...] = jnp.where(first, odd, even)
    h_t[core] = jnp.where(first, even, odd)
    remote(h_tx, h_t.at[core], send_sem.at[3], recv_sem.at[3], clip, sibling).start()

    for j in range(3):
        hcat[PAD : PAD + POS, j * C : (j + 1) * C] = shifted(hidden, j - 1, column).astype(BF16)
    mixed = dot(hcat[0:POS, :], w_space_v[0])
    for p in range(1, 3):
        mixed = mixed + dot(hcat[p * COLS : p * COLS + POS, :], w_space_v[p])
    mixed = mixed.astype(BF16)
    mixed_own[...] = mixed
    even, odd = by_parity(mixed.T)
    m_tx[...] = jnp.where(first, odd, even)
    m_t[core] = jnp.where(first, even, odd)
    remote(m_tx, m_t.at[core], send_sem.at[5], recv_sem.at[5], clip, sibling).start()

    for n in range(CHUNKS):
        rows = pl.ds(n * PIECE, PIECE)
        wait_for(cot4.at[2 + core, rows], piece_sem.at[n])
        remote(
            cot4.at[2 + core, rows], cot4.at[2 + core, rows],
            send_sem.at[4], recv_sem.at[4], clip, sibling,
        ).start()

    copies[3].wait()
    wait_for(cot4.at[0], recv_sem.at[2])
    ng_s[...] = dot(cot4[0], w_time_t[0]) + dot(cot4[1], w_time_t[1])
    hid_grad_s[...] = dot(cot4[1], w_time_t[0])
    wait_for(cot4.at[0], recv_sem.at[4])
    wait_for(cot4.at[0], send_sem.at[4])

    @pl.when(q == CHIPS - 1)
    def _():
        cot4[2] = jnp.zeros((POS, C), BF16)
        cot4[3] = jnp.zeros((POS, C), BF16)

    def scatter(tx, rx, n):
        for i, (by_x, by_y) in enumerate(PLANE_ORDER):
            x = lax.rem(2 * xh + lax.rem(q, 2) + by_x, 2 * XH)
            y = lax.rem(q // 2 + by_y, CHIPS // 2)
            xh_to, q_to = x // 2, 2 * y + lax.rem(x, 2)
            remote(
                tx.at[xh_to * CHIPS + q_to], rx.at[i], send_sem.at[n], recv_sem.at[n],
                xh_to * ZS + z, 2 * q_to + core,
            ).start()

    pl.semaphore_wait(known.at[0], 2)
    tell(1)
    wait_for(m_t.at[0], recv_sem.at[5])
    for k in range(3):
        total = (dot(m_t[0], cot4[k]) + dot(m_t[1], cot4[k + 1])).astype(BF16)
        for half in range(2):
            for to in range(CHIPS):
                rs_tx_b[half * CHIPS + to, k] = total[
                    to * 16 : to * 16 + 16, half * 128 : half * 128 + 128
                ]

    pl.semaphore_wait(known.at[3], 1)
    scatter(rs_tx_b, rs_rx_b, 7)

    for a in range(2):
        if a == 0:
            mg = ng_s[...] + dot(cot4[2], w_time_t[2])
        else:
            mg = hid_grad_s[...] + dot(cot4[2], w_time_t[1]) + dot(cot4[3], w_time_t[2])
        mg = mg.astype(BF16).astype(F32)
        for j in range(3):
            mgcat[a, PAD : PAD + POS, j * C : (j + 1) * C] = shifted(mg, 1 - j, column).astype(BF16)

    wait_for(h_t.at[0], recv_sem.at[3])
    for p in range(3):
        rows = pl.ds((2 - p) * COLS, POS)
        total = dot(h_t[0], mgcat[0, rows, :]) + dot(h_t[1], mgcat[1, rows, :])
        total = total.astype(BF16)
        for half in range(2):
            for to in range(CHIPS):
                for j in range(3):
                    block = total[
                        to * 16 : to * 16 + 16, j * C + half * 128 : j * C + half * 128 + 128
                    ]
                    if p < 2:
                        rs_tx_a[half * CHIPS + to, 3 * p + j] = block
                    else:
                        rs_tx_c[half * CHIPS + to, j] = block
        if p == 1:
            scatter(rs_tx_a, rs_rx_a, 6)
    scatter(rs_tx_c, rs_rx_c, 13)
    pl.semaphore_wait(known.at[1], 2)
    tell(2)

    hidden_grad = dot(mgcat[core, 2 * COLS : 2 * COLS + POS, :], w_space_t[0])
    for p in range(1, 3):
        rows = pl.ds((2 - p) * COLS, POS)
        hidden_grad = hidden_grad + dot(mgcat[core, rows, :], w_space_t[p])
    act = act_s[...]
    s = 1.0 / (1.0 + jnp.exp(-act))
    ng = hidden_grad * s * (1.0 + act * (1.0 - s)) * gain[...]
    ng_s[...] = ng
    normed = (clips_v[...].astype(F32) - center) * inv_std
    mean_tx[:, 0:C] = group_spread(jnp.sum(ng, axis=0, keepdims=True))
    mean_tx[:, C : 2 * C] = group_spread(jnp.sum(ng * normed, axis=0, keepdims=True))

    for i, mate in enumerate(mates):
        remote(mean_tx, mean_rx.at[i], send_sem.at[9], recv_sem.at[9], clip, mate).start()

    me = xh * CHIPS + q

    def along_z(first_tap, count):
        for tap in range(first_tap, first_tap + count):
            for half in range(2):
                to = tap % HALF + HALF * half

                @pl.when(to != z)
                def _(tap=tap, to=to):
                    n = tap // HALF
                    remote(
                        z_tx.at[tap], z_rx.at[n * ZS + z], send_sem.at[10], recv_sem.at[10 + 4 * n],
                        xh * ZS + to, frame,
                    ).start()

    def plane_sums(tx, rx, n, first_tap, count):
        wait_for(rx, recv_sem.at[n])
        for k in range(count):
            total = tx[me, k].astype(F32)
            for i in range(XH * CHIPS - 1):
                total = total + rx[i, k].astype(F32)
            z_tx[first_tap + k] = total

    plane_sums(rs_tx_b, rs_rx_b, 7, 9, 3)
    pl.semaphore_wait(known.at[2], 2)
    along_z(9, 3)
    plane_sums(rs_tx_a, rs_rx_a, 6, 0, 6)
    along_z(0, 6)
    plane_sums(rs_tx_c, rs_rx_c, 13, 6, 3)
    along_z(6, 3)

    remote(mixed_own, mixed_halo, send_sem.at[8], recv_sem.at[8], clip, after).start()

    wait_for(mean_rx, recv_sem.at[9])
    both = mean_tx[...]
    for i in range(FRAMES - 1):
        both = both + mean_rx[i]
    both = both / members
    m1, m2 = both[:, 0:C], both[:, C : 2 * C]
    normed = (clips_v[...].astype(F32) - center) * inv_std
    grad_v[...] = (
        cot4[core].astype(F32) + inv_std * (ng_s[...] - m1 - normed * m2)
    ).astype(BF16)
    grad_copy = pltpu.make_async_copy(grad_v, grad_out, local_sem.at[6])
    grad_copy.start()

    scale = 1.0 / math.sqrt(XH * ZS * FRAMES * POS)
    rest = lax.rem(z, HALF)

    def finish(n):
        tap = rest + HALF * n
        wait_for(z_rx.at[pl.ds(0, ZS - 1)], recv_sem.at[10 + 4 * n])
        z_rx[n * ZS + z] = z_tx[tap]
        total = z_rx[n * ZS]
        for i in range(1, ZS):
            total = total + z_rx[n * ZS + i]
        done = (total * scale).astype(BF16)
        fin_tx[n] = done
        gathered[tap * 2 + xh] = done

        def hand(clip_to):
            remote(
                fin_tx.at[n], gathered.at[tap * 2 + xh], send_sem.at[12], recv_sem.at[12],
                clip_to, frame,
            ).start()

        for step in (-4, 3, -3, 2, -2, 1, -1):
            to = lax.rem(z + step + ZS, ZS)
            hand((1 - xh) * ZS + to)
            hand(xh * ZS + to)
        hand(other)

    @pl.when(rest < TAPS - HALF)
    def _():
        finish(1)

    finish(0)

    wait_for(mixed_halo, recv_sem.at[8])

    @pl.when(core == 0)
    def _():
        remote(mixed_own, mixed_sib, send_sem.at[11], recv_sem.at[11], clip, sibling).start()

    @pl.when(core == 1)
    def _():
        remote(mixed_halo, mixed_sib, send_sem.at[11], recv_sem.at[11], clip, sibling).start()

    temporal = dot(mixed_own[...], w_time_v[0])
    temporal = temporal + jnp.where(q > 0, dot(mixed_halo[...], w_time_v[2]), 0.0)
    wait_for(mixed_sib, recv_sem.at[11])
    temporal = temporal + jnp.where(frame > 0, dot(mixed_sib[...], w_time_v[1]), 0.0)
    result_v[...] = (clips_v[...].astype(F32) + temporal.astype(BF16).astype(F32)).astype(BF16)
    result_copy = pltpu.make_async_copy(result_v, result_out, local_sem.at[7])
    result_copy.start()

    @pl.when(rest < TAPS - HALF)
    def _():
        wait_for(gathered.at[pl.ds(0, 2 * TAPS - 2)], recv_sem.at[12])
        wait_for(gathered.at[pl.ds(0, 2 * (ZS - 1))], send_sem.at[12])
        wait_for(z_rx.at[pl.ds(0, 2 * TAPS - 2)], send_sem.at[10])

    @pl.when(rest >= TAPS - HALF)
    def _():
        wait_for(gathered.at[pl.ds(0, 2 * TAPS - 1)], recv_sem.at[12])
        wait_for(gathered.at[pl.ds(0, ZS - 1)], send_sem.at[12])
        wait_for(z_rx.at[pl.ds(0, 2 * TAPS - 1)], send_sem.at[10])

    for k in range(TAPS):
        for half in range(2):
            taps_v[k, :, half * 128 : half * 128 + 128] = gathered[2 * k + half]
    taps_copy = pltpu.make_async_copy(taps_v, taps_out, local_sem.at[8])
    taps_copy.start()

    wait_for(stat_rx, send_sem.at[0])
    wait_for(cot4.at[0], send_sem.at[1])
    wait_for(cot4.at[0], send_sem.at[2])
    wait_for(h_tx, send_sem.at[3])
    wait_for(m_tx, send_sem.at[5])
    wait_for(rs_rx_a, send_sem.at[6])
    wait_for(rs_rx_b, send_sem.at[7])
    wait_for(rs_rx_c, send_sem.at[13])
    wait_for(mixed_own, send_sem.at[8])
    wait_for(mean_rx, send_sem.at[9])
    wait_for(mixed_own, send_sem.at[11])
    for copy in (grad_copy, result_copy, taps_copy):
        copy.wait()


def write_out(result, grad, taps, result_out, grad_out, space_out, time_out, *scratch):
    result_v, grad_v, taps_v, in_sem, out_sem = scratch
    moves = [(taps, taps_v, ((0, 9, space_out), (9, 3, time_out)))]
    half = POS // 2
    for source, held, target in ((result, result_v, result_out), (grad, grad_v, grad_out)):
        for n in range(2):
            rows = pl.ds(n * half, half)
            moves.append((source.at[rows], held.at[rows], ((0, half, target.at[rows]),)))
    into = [
        pltpu.make_async_copy(source, held, in_sem.at[n])
        for n, (source, held, _) in enumerate(moves)
    ]
    for copy in into:
        copy.start()
    back = []
    for copy, (_, held, parts) in zip(into, moves):
        copy.wait()
        for first, count, target in parts:
            back.append(
                pltpu.make_async_copy(held.at[pl.ds(first, count)], target, out_sem.at[len(back)])
            )
            back[-1].start()
    for copy in back:
        copy.wait()


def per_device(clips, cotangent, norm_gain, norm_shift, w_spatial, w_time):
    hbm = pl.BlockSpec(memory_space=pltpu.HBM)
    blocks = pl.pallas_call(
        kernel,
        name="video_block",
        out_shape=(
            jax.ShapeDtypeStruct((POS, C), BF16),
            jax.ShapeDtypeStruct((POS, C), BF16),
            jax.ShapeDtypeStruct((TAPS, 16, C), BF16),
        ),
        in_specs=[hbm] * 6,
        out_specs=(hbm, hbm, hbm),
        scratch_shapes=[
            pltpu.VMEM((POS, C), BF16),
            pltpu.VMEM((4, POS, C), BF16),
            pltpu.VMEM((3, 3 * C, C), BF16),
            pltpu.VMEM((3, C, C), BF16),
            pltpu.VMEM((3, 3 * C, C), BF16),
            pltpu.VMEM((3, C, C), BF16),
            pltpu.VMEM((POS + 2 * PAD, 3 * C), BF16),
            pltpu.VMEM((2, POS + 2 * PAD, 3 * C), BF16),
            pltpu.VMEM((POS, C), F32),
            pltpu.VMEM((POS, C), F32),
            pltpu.VMEM((POS, C), F32),
            pltpu.VMEM((2, 128, POS), BF16),
            pltpu.VMEM((128, POS), BF16),
            pltpu.VMEM((2, 128, POS), BF16),
            pltpu.VMEM((128, POS), BF16),
            pltpu.VMEM((POS, C), BF16),
            pltpu.VMEM((POS, C), BF16),
            pltpu.VMEM((POS, C), BF16),
            pltpu.VMEM((1, 2 * C), F32),
            pltpu.VMEM((FRAMES - 1, 1, 2 * C), F32),
            pltpu.VMEM((1, 2 * C), F32),
            pltpu.VMEM((FRAMES - 1, 1, 2 * C), F32),
            pltpu.VMEM((XH * CHIPS, 6, 16, 128), BF16),
            pltpu.VMEM((XH * CHIPS - 1, 6, 16, 128), BF16),
            pltpu.VMEM((XH * CHIPS, 3, 16, 128), BF16),
            pltpu.VMEM((XH * CHIPS - 1, 3, 16, 128), BF16),
            pltpu.VMEM((XH * CHIPS, 3, 16, 128), BF16),
            pltpu.VMEM((XH * CHIPS - 1, 3, 16, 128), BF16),
            pltpu.VMEM((TAPS, 16, 128), F32),
            pltpu.VMEM((2 * ZS, 16, 128), F32),
            pltpu.VMEM((2, 16, 128), BF16),
            pltpu.VMEM((XH * ZS - 1, 16, 128), BF16),
            pltpu.VMEM((1, C), F32),
            pltpu.VMEM((1, C), F32),
            pltpu.VMEM((POS, C), BF16),
            pltpu.VMEM((POS, C), BF16),
            pltpu.VMEM((TAPS, 16, C), BF16),
            pltpu.SemaphoreType.DMA((9,)),
            pltpu.SemaphoreType.DMA((15,)),
            pltpu.SemaphoreType.DMA((15,)),
            pltpu.SemaphoreType.DMA((CHUNKS,)),
            pltpu.SemaphoreType.REGULAR((4,)),
        ],
        compiler_params=pltpu.CompilerParams(
            collective_id=0, has_side_effects=True, vmem_limit_bytes=VMEM_BYTES
        ),
    )(
        clips.reshape(POS, C),
        cotangent.reshape(POS, C),
        norm_gain.reshape(1, C),
        norm_shift.reshape(1, C),
        w_spatial.reshape(3, 3 * C, C),
        w_time,
    )
    result, grad, space, time = pl.pallas_call(
        write_out,
        name="write_out",
        out_shape=(
            jax.ShapeDtypeStruct((POS, C), BF16),
            jax.ShapeDtypeStruct((POS, C), BF16),
            jax.ShapeDtypeStruct((9, 16, C), BF16),
            jax.ShapeDtypeStruct((3, 16, C), BF16),
        ),
        in_specs=[hbm, hbm, hbm],
        out_specs=(hbm, hbm, hbm, hbm),
        scratch_shapes=[
            pltpu.VMEM((POS, C), BF16),
            pltpu.VMEM((POS, C), BF16),
            pltpu.VMEM((TAPS, 16, C), BF16),
            pltpu.SemaphoreType.DMA((5,)),
            pltpu.SemaphoreType.DMA((6,)),
        ],
        compiler_params=pltpu.CompilerParams(vmem_limit_bytes=VMEM_BYTES),
    )(*blocks)
    return (
        result.reshape(clips.shape),
        grad.reshape(clips.shape),
        space.reshape(3, 3, 16, C),
        time,
    )


def solution(mesh):
    placed = (
        P("clip", "frame", None, None, None),
        P("clip", "frame", None, None, None),
        P(),
        P(),
        P(),
        P(),
    )
    return jax.shard_map(
        per_device,
        mesh=mesh,
        in_specs=placed,
        out_specs=(
            P("clip", "frame", None, None, None),
            P("clip", "frame", None, None, None),
            P(None, None, "frame", None),
            P(None, "frame", None),
        ),
        check_vma=False,
    )
```

```python
import functools
import math

import jax
import jax.numpy as jnp
from jax import lax
from jax.experimental import pallas as pl
from jax.experimental.pallas import tpu as pltpu
from jax.sharding import PartitionSpec as P

GROUPS = 32
EPSILON = 1e-05
MESH = pl.DeviceIdType.MESH
F32 = jnp.float32
BF16 = jnp.bfloat16

ROWS, COLS, C = 16, 32, 256
POS = ROWS * COLS
PAD = COLS
TAPS = 12
VMEM_BYTES = 60 * 2**20

FRAME_ORDER = (
    (2, 1, 0), (2, 1, 1), (2, 0, 0), (2, 0, 1), (1, 1, 0), (1, 1, 1), (3, 1, 0), (3, 1, 1),
    (1, 0, 0), (1, 0, 1), (3, 0, 0), (3, 0, 1), (0, 1, 0), (0, 1, 1), (0, 0, 1),
)

PLANE_ORDER = (
    (2, 2), (2, 1), (1, 2), (2, 3), (3, 2), (1, 1), (3, 3), (1, 3),
    (3, 1), (2, 0), (0, 2), (1, 0), (0, 1), (3, 0), (0, 3),
)
CHUNKS = 4
PIECE = POS // CHUNKS

ZS, XH, CHIPS = 16, 2, 8
HALF = ZS // 2
FRAMES = 2 * CHIPS


def dot(a, b):
    return jnp.dot(a, b, preferred_element_type=F32)


def remote(src, dst, send_sem, recv_sem, clip, frame):
    return pltpu.make_async_remote_copy(
        src_ref=src,
        dst_ref=dst,
        send_sem=send_sem,
        recv_sem=recv_sem,
        device_id=(clip, frame),
        device_id_type=MESH,
    )


def wait_for(ref, sem):
    pltpu.make_async_copy(ref, ref, sem).wait()


def loop(count, body):
    def step(i, carry):
        body(i)
        return carry

    lax.fori_loop(0, count, step, 0)


def far_first(i):
    return (HALF - (i + 1) // 2) * (1 - 2 * lax.rem(i + 1, 2))


def group_spread(row):
    lane = lax.broadcasted_iota(jnp.int32, row.shape, 1)
    for bit in (1, 2, 4):
        up = pltpu.roll(row, bit, 1)
        down = pltpu.roll(row, row.shape[1] - bit, 1)
        row = row + jnp.where((lane & bit) != 0, up, down)
    return row


def shifted(values, by, column):
    if by == 0:
        return values
    rolled = pltpu.roll(values, (-by) % values.shape[0], 0)
    edge = 0 if by < 0 else COLS - 1
    return jnp.where(column == edge, 0.0, rolled)


def by_parity(columns):
    strips = columns.reshape(8, 2, 16, columns.shape[1])
    return (
        strips[:, 0].reshape(128, columns.shape[1]),
        strips[:, 1].reshape(128, columns.shape[1]),
    )


def kernel(
    clips, cot, gain_in, shift_in, w_space, w_time,
    result_out, grad_out, taps_out,
    clips_v, cot4, w_space_v, w_time_v, w_space_t, w_time_t,
    hcat, mgcat, act_s, hid_grad_s, ng_s, h_t, h_tx, m_t, m_tx, mixed_own, mixed_halo, mixed_sib,
    stat_tx, stat_rx, mean_tx, mean_rx,
    rs_tx_a, rs_rx_a, rs_tx_b, rs_rx_b, rs_tx_c, rs_rx_c, rs_tx_d, rs_rx_d, z_tx, z_rx, fin_tx, gathered,
    gain, shift, result_v, grad_v, taps_v, local_sem, send_sem, recv_sem, piece_sem, known,
):
    clip = lax.axis_index("clip")
    frame = lax.axis_index("frame")
    xh, z = clip // ZS, lax.rem(clip, ZS)
    q, core = frame // 2, lax.rem(frame, 2)
    sibling = frame + 1 - 2 * core
    members = FRAMES * POS * (C // GROUPS)

    barrier = pltpu.get_barrier_semaphore()

    def greet(clip_to, frame_to):
        pl.semaphore_signal(
            barrier, inc=1, device_id=(clip_to, frame_to), device_id_type=MESH
        )

    def along(by):
        return xh * ZS + lax.rem(z + by + ZS, ZS)

    def tell(step):
        for by in (-(2**step), 2**step):
            pl.semaphore_signal(
                known.at[step], inc=1, device_id=(along(by), frame), device_id_type=MESH
            )

    y, x_lo = q // 2, lax.rem(q, 2)
    other = (1 - xh) * ZS + z
    mates = [
        4 * lax.rem(y + by_y, CHIPS // 2)
        + 2 * (1 - x_lo if by_x else x_lo)
        + (1 - core if by_core else core)
        for by_y, by_x, by_core in FRAME_ORDER
    ]
    for mate in mates:
        greet(clip, mate)
    greet(other, frame)
    greet(along(-1), frame)
    greet(along(1), frame)

    copies = [
        pltpu.make_async_copy(clips, clips_v, local_sem.at[0]),
        pltpu.make_async_copy(w_time, w_time_v, local_sem.at[1]),
        pltpu.make_async_copy(w_space, w_space_v, local_sem.at[2]),
        pltpu.make_async_copy(cot, cot4.at[core], local_sem.at[3]),
        pltpu.make_async_copy(gain_in, gain, local_sem.at[4]),
        pltpu.make_async_copy(shift_in, shift, local_sem.at[5]),
    ]
    for copy in copies:
        copy.start()

    zero = jnp.zeros((PAD, 3 * C), BF16)
    for buffer in (hcat, mgcat.at[0], mgcat.at[1]):
        buffer[0:PAD, :] = zero
        buffer[PAD + POS : PAD + POS + PAD, :] = zero

    copies[0].wait()
    values = clips_v[...].astype(F32)
    own_sum = group_spread(jnp.sum(values, axis=0, keepdims=True))
    own_mean = own_sum / (POS * (C // GROUPS))
    offset = values - own_mean
    own_squares = group_spread(jnp.sum(offset * offset, axis=0, keepdims=True))
    stat_tx[:, 0:C] = own_sum
    stat_tx[:, C : 2 * C] = own_squares
    pl.semaphore_wait(barrier, FRAMES - 1 + 3)

    for i, mate in enumerate(mates):
        remote(stat_tx, stat_rx.at[i], send_sem.at[0], recv_sem.at[0], clip, mate).start()

    before = lax.rem(frame + FRAMES - 2, FRAMES)
    after = lax.rem(frame + 2, FRAMES)
    for n in range(CHUNKS):
        rows = pl.ds(n * PIECE, PIECE)
        remote(
            cot.at[rows], cot4.at[2 + core, rows], send_sem.at[1], piece_sem.at[n], clip, before
        ).start()
    remote(cot, cot4.at[core], send_sem.at[2], recv_sem.at[2], clip, sibling).start()

    tell(0)
    pl.semaphore_signal(known.at[3], inc=1, device_id=(other, frame), device_id_type=MESH)

    copies[1].wait()
    for k in range(3):
        w_time_t[k] = w_time_v[k].T
    copies[4].wait()
    copies[5].wait()
    copies[2].wait()
    for p in range(3):
        for j in range(3):
            w_space_t[p, j * C : (j + 1) * C, :] = w_space_v[p, j * C : (j + 1) * C, :].T

    wait_for(stat_rx, recv_sem.at[0])
    own = stat_tx[...]
    sums = own[:, 0:C]
    squares = own[:, C : 2 * C]
    for i in range(FRAMES - 1):
        sums = sums + stat_rx[i, :, 0:C]
        squares = squares + stat_rx[i, :, C : 2 * C]
    center = sums / members
    part = POS * (C // GROUPS)
    away = own[:, 0:C] / part - center
    spread = away * away
    for i in range(FRAMES - 1):
        away = stat_rx[i, :, 0:C] / part - center
        spread = spread + away * away
    variance = (squares + part * spread) / members
    inv_std = lax.rsqrt(variance + EPSILON)

    column = lax.rem(lax.broadcasted_iota(jnp.int32, (POS, C), 0), COLS)
    normed = (clips_v[...].astype(F32) - center) * inv_std
    act = normed * gain[...] + shift[...]
    act_s[...] = act
    hidden = act / (1.0 + jnp.exp(-act))
    even, odd = by_parity(hidden.astype(BF16).T)
    first = core == 0
    h_tx[...] = jnp.where(first, odd, even)
    h_t[core] = jnp.where(first, even, odd)
    remote(h_tx, h_t.at[core], send_sem.at[3], recv_sem.at[3], clip, sibling).start()

    for j in range(3):
        hcat[PAD : PAD + POS, j * C : (j + 1) * C] = shifted(hidden, j - 1, column).astype(BF16)
    mixed = dot(hcat[0:POS, :], w_space_v[0])
    for p in range(1, 3):
        mixed = mixed + dot(hcat[p * COLS : p * COLS + POS, :], w_space_v[p])
    mixed = mixed.astype(BF16)
    mixed_own[...] = mixed
    even, odd = by_parity(mixed.T)
    m_tx[...] = jnp.where(first, odd, even)
    m_t[core] = jnp.where(first, even, odd)
    remote(m_tx, m_t.at[core], send_sem.at[5], recv_sem.at[5], clip, sibling).start()

    for n in range(CHUNKS):
        rows = pl.ds(n * PIECE, PIECE)
        wait_for(cot4.at[2 + core, rows], piece_sem.at[n])
        remote(
            cot4.at[2 + core, rows], cot4.at[2 + core, rows],
            send_sem.at[4], recv_sem.at[4], clip, sibling,
        ).start()

    copies[3].wait()
    wait_for(cot4.at[0], recv_sem.at[2])
    ng_s[...] = dot(cot4[0], w_time_t[0]) + dot(cot4[1], w_time_t[1])
    hid_grad_s[...] = dot(cot4[1], w_time_t[0])
    wait_for(cot4.at[0], recv_sem.at[4])
    wait_for(cot4.at[0], send_sem.at[4])

    @pl.when(q == CHIPS - 1)
    def _():
        cot4[2] = jnp.zeros((POS, C), BF16)
        cot4[3] = jnp.zeros((POS, C), BF16)

    def scatter(tx, rx, n):
        for i, (by_x, by_y) in enumerate(PLANE_ORDER):
            x = lax.rem(2 * xh + lax.rem(q, 2) + by_x, 2 * XH)
            y = lax.rem(q // 2 + by_y, CHIPS // 2)
            xh_to, q_to = x // 2, 2 * y + lax.rem(x, 2)
            remote(
                tx.at[xh_to * CHIPS + q_to], rx.at[i], send_sem.at[n], recv_sem.at[n],
                xh_to * ZS + z, 2 * q_to + core,
            ).start()

    pl.semaphore_wait(known.at[0], 2)
    tell(1)
    wait_for(m_t.at[0], recv_sem.at[5])
    for k in range(3):
        total = (dot(m_t[0], cot4[k]) + dot(m_t[1], cot4[k + 1])).astype(BF16)
        for half in range(2):
            for to in range(CHIPS):
                rs_tx_b[half * CHIPS + to, k] = total[
                    to * 16 : to * 16 + 16, half * 128 : half * 128 + 128
                ]

    pl.semaphore_wait(known.at[3], 1)
    scatter(rs_tx_b, rs_rx_b, 7)

    for a in range(2):
        if a == 0:
            mg = ng_s[...] + dot(cot4[2], w_time_t[2])
        else:
            mg = hid_grad_s[...] + dot(cot4[2], w_time_t[1]) + dot(cot4[3], w_time_t[2])
        mg = mg.astype(BF16).astype(F32)
        for j in range(3):
            mgcat[a, PAD : PAD + POS, j * C : (j + 1) * C] = shifted(mg, 1 - j, column).astype(BF16)

    wait_for(h_t.at[0], recv_sem.at[3])
    row_groups = ((rs_tx_a, rs_rx_a, 6), (rs_tx_c, rs_rx_c, 13), (rs_tx_d, rs_rx_d, 15))
    for p, (tx, rx, n) in enumerate(row_groups):
        rows = pl.ds((2 - p) * COLS, POS)
        total = dot(h_t[0], mgcat[0, rows, :]) + dot(h_t[1], mgcat[1, rows, :])
        total = total.astype(BF16)
        for half in range(2):
            for to in range(CHIPS):
                for j in range(3):
                    tx[half * CHIPS + to, j] = total[
                        to * 16 : to * 16 + 16, j * C + half * 128 : j * C + half * 128 + 128
                    ]
        scatter(tx, rx, n)
    pl.semaphore_wait(known.at[1], 2)
    tell(2)

    hidden_grad = dot(mgcat[core, 2 * COLS : 2 * COLS + POS, :], w_space_t[0])
    for p in range(1, 3):
        rows = pl.ds((2 - p) * COLS, POS)
        hidden_grad = hidden_grad + dot(mgcat[core, rows, :], w_space_t[p])
    act = act_s[...]
    s = 1.0 / (1.0 + jnp.exp(-act))
    ng = hidden_grad * s * (1.0 + act * (1.0 - s)) * gain[...]
    ng_s[...] = ng
    normed = (clips_v[...].astype(F32) - center) * inv_std
    mean_tx[:, 0:C] = group_spread(jnp.sum(ng, axis=0, keepdims=True))
    mean_tx[:, C : 2 * C] = group_spread(jnp.sum(ng * normed, axis=0, keepdims=True))

    for i, mate in enumerate(mates):
        remote(mean_tx, mean_rx.at[i], send_sem.at[9], recv_sem.at[9], clip, mate).start()

    me = xh * CHIPS + q

    def along_z(first_tap, count):
        def send(i):
            to = lax.rem(z + ZS + far_first(i), ZS)
            for n in range(2):
                tap = lax.rem(to, HALF) + HALF * n

                @pl.when((tap >= first_tap) & (tap < first_tap + count))
                def _(n=n, tap=tap):
                    remote(
                        z_tx.at[tap], z_rx.at[n * ZS + z], send_sem.at[10], recv_sem.at[10 + 4 * n],
                        xh * ZS + to, frame,
                    ).start()

        loop(ZS - 1, send)

    def plane_sums(tx, rx, n, first_tap, count):
        wait_for(rx, recv_sem.at[n])
        for k in range(count):
            total = tx[me, k].astype(F32)
            for i in range(XH * CHIPS - 1):
                total = total + rx[i, k].astype(F32)
            z_tx[first_tap + k] = total

    plane_sums(rs_tx_b, rs_rx_b, 7, 9, 3)
    pl.semaphore_wait(known.at[2], 2)
    along_z(9, 3)
    for p, (tx, rx, n) in enumerate(row_groups):
        plane_sums(tx, rx, n, 3 * p, 3)
        along_z(3 * p, 3)

    remote(mixed_own, mixed_halo, send_sem.at[8], recv_sem.at[8], clip, after).start()

    wait_for(mean_rx, recv_sem.at[9])
    both = mean_tx[...]
    for i in range(FRAMES - 1):
        both = both + mean_rx[i]
    both = both / members
    m1, m2 = both[:, 0:C], both[:, C : 2 * C]
    normed = (clips_v[...].astype(F32) - center) * inv_std
    grad_v[...] = (
        cot4[core].astype(F32) + inv_std * (ng_s[...] - m1 - normed * m2)
    ).astype(BF16)
    grad_copy = pltpu.make_async_copy(grad_v, grad_out, local_sem.at[6])
    grad_copy.start()

    scale = 1.0 / math.sqrt(XH * ZS * FRAMES * POS)
    rest = lax.rem(z, HALF)

    def finish(n):
        tap = rest + HALF * n
        wait_for(z_rx.at[pl.ds(0, ZS - 1)], recv_sem.at[10 + 4 * n])
        z_rx[n * ZS + z] = z_tx[tap]
        total = z_rx[n * ZS]
        for i in range(1, ZS):
            total = total + z_rx[n * ZS + i]
        done = (total * scale).astype(BF16)
        fin_tx[n] = done
        gathered[tap * 2 + xh] = done

        def hand(clip_to):
            remote(
                fin_tx.at[n], gathered.at[tap * 2 + xh], send_sem.at[12], recv_sem.at[12],
                clip_to, frame,
            ).start()

        for step in (-4, 3, -3, 2, -2, 1, -1):
            to = lax.rem(z + step + ZS, ZS)
            hand((1 - xh) * ZS + to)
            hand(xh * ZS + to)
        hand(other)

    @pl.when(rest < TAPS - HALF)
    def _():
        finish(1)

    finish(0)

    wait_for(mixed_halo, recv_sem.at[8])

    @pl.when(core == 0)
    def _():
        remote(mixed_own, mixed_sib, send_sem.at[11], recv_sem.at[11], clip, sibling).start()

    @pl.when(core == 1)
    def _():
        remote(mixed_halo, mixed_sib, send_sem.at[11], recv_sem.at[11], clip, sibling).start()

    temporal = dot(mixed_own[...], w_time_v[0])
    temporal = temporal + jnp.where(q > 0, dot(mixed_halo[...], w_time_v[2]), 0.0)
    wait_for(mixed_sib, recv_sem.at[11])
    temporal = temporal + jnp.where(frame > 0, dot(mixed_sib[...], w_time_v[1]), 0.0)
    result_v[...] = (clips_v[...].astype(F32) + temporal.astype(BF16).astype(F32)).astype(BF16)
    result_copy = pltpu.make_async_copy(result_v, result_out, local_sem.at[7])
    result_copy.start()

    @pl.when(rest < TAPS - HALF)
    def _():
        wait_for(gathered.at[pl.ds(0, 2 * TAPS - 2)], recv_sem.at[12])
        wait_for(gathered.at[pl.ds(0, 2 * (ZS - 1))], send_sem.at[12])
        wait_for(z_rx.at[pl.ds(0, 2 * TAPS - 2)], send_sem.at[10])

    @pl.when(rest >= TAPS - HALF)
    def _():
        wait_for(gathered.at[pl.ds(0, 2 * TAPS - 1)], recv_sem.at[12])
        wait_for(gathered.at[pl.ds(0, ZS - 1)], send_sem.at[12])
        wait_for(z_rx.at[pl.ds(0, 2 * TAPS - 1)], send_sem.at[10])

    for k in range(TAPS):
        for half in range(2):
            taps_v[k, :, half * 128 : half * 128 + 128] = gathered[2 * k + half]
    taps_copy = pltpu.make_async_copy(taps_v, taps_out, local_sem.at[8])
    taps_copy.start()

    wait_for(stat_rx, send_sem.at[0])
    wait_for(cot4.at[0], send_sem.at[1])
    wait_for(cot4.at[0], send_sem.at[2])
    wait_for(h_tx, send_sem.at[3])
    wait_for(m_tx, send_sem.at[5])
    wait_for(rs_rx_a, send_sem.at[6])
    wait_for(rs_rx_b, send_sem.at[7])
    wait_for(rs_rx_c, send_sem.at[13])
    wait_for(rs_rx_d, send_sem.at[15])
    wait_for(mixed_own, send_sem.at[8])
    wait_for(mean_rx, send_sem.at[9])
    wait_for(mixed_own, send_sem.at[11])
    for copy in (grad_copy, result_copy, taps_copy):
        copy.wait()


def write_out(result, grad, taps, result_out, grad_out, space_out, time_out, *scratch):
    result_v, grad_v, taps_v, in_sem, out_sem = scratch
    moves = [(taps, taps_v, ((0, 9, space_out), (9, 3, time_out)))]
    half = POS // 2
    for source, held, target in ((result, result_v, result_out), (grad, grad_v, grad_out)):
        for n in range(2):
            rows = pl.ds(n * half, half)
            moves.append((source.at[rows], held.at[rows], ((0, half, target.at[rows]),)))
    into = [
        pltpu.make_async_copy(source, held, in_sem.at[n])
        for n, (source, held, _) in enumerate(moves)
    ]
    for copy in into:
        copy.start()
    back = []
    for copy, (_, held, parts) in zip(into, moves):
        copy.wait()
        for first, count, target in parts:
            back.append(
                pltpu.make_async_copy(held.at[pl.ds(first, count)], target, out_sem.at[len(back)])
            )
            back[-1].start()
    for copy in back:
        copy.wait()


def per_device(clips, cotangent, norm_gain, norm_shift, w_spatial, w_time):
    hbm = pl.BlockSpec(memory_space=pltpu.HBM)
    blocks = pl.pallas_call(
        kernel,
        name="video_block",
        out_shape=(
            jax.ShapeDtypeStruct((POS, C), BF16),
            jax.ShapeDtypeStruct((POS, C), BF16),
            jax.ShapeDtypeStruct((TAPS, 16, C), BF16),
        ),
        in_specs=[hbm] * 6,
        out_specs=(hbm, hbm, hbm),
        scratch_shapes=[
            pltpu.VMEM((POS, C), BF16),
            pltpu.VMEM((4, POS, C), BF16),
            pltpu.VMEM((3, 3 * C, C), BF16),
            pltpu.VMEM((3, C, C), BF16),
            pltpu.VMEM((3, 3 * C, C), BF16),
            pltpu.VMEM((3, C, C), BF16),
            pltpu.VMEM((POS + 2 * PAD, 3 * C), BF16),
            pltpu.VMEM((2, POS + 2 * PAD, 3 * C), BF16),
            pltpu.VMEM((POS, C), F32),
            pltpu.VMEM((POS, C), F32),
            pltpu.VMEM((POS, C), F32),
            pltpu.VMEM((2, 128, POS), BF16),
            pltpu.VMEM((128, POS), BF16),
            pltpu.VMEM((2, 128, POS), BF16),
            pltpu.VMEM((128, POS), BF16),
            pltpu.VMEM((POS, C), BF16),
            pltpu.VMEM((POS, C), BF16),
            pltpu.VMEM((POS, C), BF16),
            pltpu.VMEM((1, 2 * C), F32),
            pltpu.VMEM((FRAMES - 1, 1, 2 * C), F32),
            pltpu.VMEM((1, 2 * C), F32),
            pltpu.VMEM((FRAMES - 1, 1, 2 * C), F32),
            pltpu.VMEM((XH * CHIPS, 3, 16, 128), BF16),
            pltpu.VMEM((XH * CHIPS - 1, 3, 16, 128), BF16),
            pltpu.VMEM((XH * CHIPS, 3, 16, 128), BF16),
            pltpu.VMEM((XH * CHIPS - 1, 3, 16, 128), BF16),
            pltpu.VMEM((XH * CHIPS, 3, 16, 128), BF16),
            pltpu.VMEM((XH * CHIPS - 1, 3, 16, 128), BF16),
            pltpu.VMEM((XH * CHIPS, 3, 16, 128), BF16),
            pltpu.VMEM((XH * CHIPS - 1, 3, 16, 128), BF16),
            pltpu.VMEM((TAPS, 16, 128), F32),
            pltpu.VMEM((2 * ZS, 16, 128), F32),
            pltpu.VMEM((2, 16, 128), BF16),
            pltpu.VMEM((XH * ZS - 1, 16, 128), BF16),
            pltpu.VMEM((1, C), F32),
            pltpu.VMEM((1, C), F32),
            pltpu.VMEM((POS, C), BF16),
            pltpu.VMEM((POS, C), BF16),
            pltpu.VMEM((TAPS, 16, C), BF16),
            pltpu.SemaphoreType.DMA((9,)),
            pltpu.SemaphoreType.DMA((16,)),
            pltpu.SemaphoreType.DMA((16,)),
            pltpu.SemaphoreType.DMA((CHUNKS,)),
            pltpu.SemaphoreType.REGULAR((4,)),
        ],
        compiler_params=pltpu.CompilerParams(
            collective_id=0, has_side_effects=True, vmem_limit_bytes=VMEM_BYTES
        ),
    )(
        clips.reshape(POS, C),
        cotangent.reshape(POS, C),
        norm_gain.reshape(1, C),
        norm_shift.reshape(1, C),
        w_spatial.reshape(3, 3 * C, C),
        w_time,
    )
    result, grad, space, time = pl.pallas_call(
        write_out,
        name="write_out",
        out_shape=(
            jax.ShapeDtypeStruct((POS, C), BF16),
            jax.ShapeDtypeStruct((POS, C), BF16),
            jax.ShapeDtypeStruct((9, 16, C), BF16),
            jax.ShapeDtypeStruct((3, 16, C), BF16),
        ),
        in_specs=[hbm, hbm, hbm],
        out_specs=(hbm, hbm, hbm, hbm),
        scratch_shapes=[
            pltpu.VMEM((POS, C), BF16),
            pltpu.VMEM((POS, C), BF16),
            pltpu.VMEM((TAPS, 16, C), BF16),
            pltpu.SemaphoreType.DMA((5,)),
            pltpu.SemaphoreType.DMA((6,)),
        ],
        compiler_params=pltpu.CompilerParams(vmem_limit_bytes=VMEM_BYTES),
    )(*blocks)
    return (
        result.reshape(clips.shape),
        grad.reshape(clips.shape),
        space.reshape(3, 3, 16, C),
        time,
    )


def solution(mesh):
    placed = (
        P("clip", "frame", None, None, None),
        P("clip", "frame", None, None, None),
        P(),
        P(),
        P(),
        P(),
    )
    return jax.shard_map(
        per_device,
        mesh=mesh,
        in_specs=placed,
        out_specs=(
            P("clip", "frame", None, None, None),
            P("clip", "frame", None, None, None),
            P(None, None, "frame", None),
            P(None, "frame", None),
        ),
        check_vma=False,
    )
```

```python
import functools
import math

import jax
import jax.numpy as jnp
from jax import lax
from jax.experimental import pallas as pl
from jax.experimental.pallas import tpu as pltpu
from jax.sharding import PartitionSpec as P

GROUPS = 32
EPSILON = 1e-05
MESH = pl.DeviceIdType.MESH
F32 = jnp.float32
BF16 = jnp.bfloat16

ROWS, COLS, C = 16, 32, 256
POS = ROWS * COLS
PAD = COLS
TAPS = 12
VMEM_BYTES = 60 * 2**20

FRAME_ORDER = (
    (2, 1, 0), (2, 1, 1), (2, 0, 0), (2, 0, 1), (1, 1, 0), (1, 1, 1), (3, 1, 0), (3, 1, 1),
    (1, 0, 0), (1, 0, 1), (3, 0, 0), (3, 0, 1), (0, 1, 0), (0, 1, 1), (0, 0, 1),
)

PLANE_ORDER = (
    (2, 2), (2, 1), (1, 2), (2, 3), (3, 2), (1, 1), (3, 3), (1, 3),
    (3, 1), (2, 0), (0, 2), (1, 0), (0, 1), (3, 0), (0, 3),
)
CHUNKS = 4
PIECE = POS // CHUNKS

ZS, XH, CHIPS = 16, 2, 8
HALF = ZS // 2
FRAMES = 2 * CHIPS


def dot(a, b):
    return jnp.dot(a, b, preferred_element_type=F32)


def remote(src, dst, send_sem, recv_sem, clip, frame):
    return pltpu.make_async_remote_copy(
        src_ref=src,
        dst_ref=dst,
        send_sem=send_sem,
        recv_sem=recv_sem,
        device_id=(clip, frame),
        device_id_type=MESH,
    )


def wait_for(ref, sem):
    pltpu.make_async_copy(ref, ref, sem).wait()


def loop(count, body):
    def step(i, carry):
        body(i)
        return carry

    lax.fori_loop(0, count, step, 0)


def far_first(i):
    return (HALF - (i + 1) // 2) * (1 - 2 * lax.rem(i + 1, 2))


def group_spread(row):
    lane = lax.broadcasted_iota(jnp.int32, row.shape, 1)
    for bit in (1, 2, 4):
        up = pltpu.roll(row, bit, 1)
        down = pltpu.roll(row, row.shape[1] - bit, 1)
        row = row + jnp.where((lane & bit) != 0, up, down)
    return row


def shifted(values, by, column):
    if by == 0:
        return values
    rolled = pltpu.roll(values, (-by) % values.shape[0], 0)
    edge = 0 if by < 0 else COLS - 1
    return jnp.where(column == edge, 0.0, rolled)


def by_parity(columns):
    strips = columns.reshape(8, 2, 16, columns.shape[1])
    return (
        strips[:, 0].reshape(128, columns.shape[1]),
        strips[:, 1].reshape(128, columns.shape[1]),
    )


def kernel(
    clips, cot, gain_in, shift_in, w_space, w_time,
    result_out, grad_out, taps_out,
    clips_v, cot4, w_space_v, w_time_v, w_space_t, w_time_t,
    hcat, mgcat, act_s, hid_grad_s, ng_s, h_t, h_tx, m_t, m_tx, mixed_own, mixed_halo, mixed_sib,
    stat_tx, stat_rx, mean_tx, mean_rx,
    rs_tx_a, rs_rx_a, rs_tx_b, rs_rx_b, rs_tx_c, rs_rx_c, rs_tx_d, rs_rx_d, z_tx, z_rx, fin_tx, gathered,
    gain, shift, result_v, grad_v, taps_v, local_sem, send_sem, recv_sem, piece_sem, known,
):
    clip = lax.axis_index("clip")
    frame = lax.axis_index("frame")
    xh, z = clip // ZS, lax.rem(clip, ZS)
    q, core = frame // 2, lax.rem(frame, 2)
    sibling = frame + 1 - 2 * core
    members = FRAMES * POS * (C // GROUPS)

    barrier = pltpu.get_barrier_semaphore()

    def greet(clip_to, frame_to):
        pl.semaphore_signal(
            barrier, inc=1, device_id=(clip_to, frame_to), device_id_type=MESH
        )

    def along(by):
        return xh * ZS + lax.rem(z + by + ZS, ZS)

    def tell(step):
        for by in (-(2**step), 2**step):
            pl.semaphore_signal(
                known.at[step], inc=1, device_id=(along(by), frame), device_id_type=MESH
            )

    y, x_lo = q // 2, lax.rem(q, 2)
    other = (1 - xh) * ZS + z
    mates = [
        4 * lax.rem(y + by_y, CHIPS // 2)
        + 2 * (1 - x_lo if by_x else x_lo)
        + (1 - core if by_core else core)
        for by_y, by_x, by_core in FRAME_ORDER
    ]
    for mate in mates:
        greet(clip, mate)
    greet(other, frame)
    greet(along(-1), frame)
    greet(along(1), frame)

    copies = [
        pltpu.make_async_copy(clips, clips_v, local_sem.at[0]),
        pltpu.make_async_copy(w_time, w_time_v, local_sem.at[1]),
        pltpu.make_async_copy(w_space, w_space_v, local_sem.at[2]),
        pltpu.make_async_copy(cot, cot4.at[core], local_sem.at[3]),
        pltpu.make_async_copy(gain_in, gain, local_sem.at[4]),
        pltpu.make_async_copy(shift_in, shift, local_sem.at[5]),
    ]
    for copy in copies:
        copy.start()

    zero = jnp.zeros((PAD, 3 * C), BF16)
    for buffer in (hcat, mgcat.at[0], mgcat.at[1]):
        buffer[0:PAD, :] = zero
        buffer[PAD + POS : PAD + POS + PAD, :] = zero

    copies[0].wait()
    values = clips_v[...].astype(F32)
    own_sum = group_spread(jnp.sum(values, axis=0, keepdims=True))
    own_mean = own_sum / (POS * (C // GROUPS))
    offset = values - own_mean
    own_squares = group_spread(jnp.sum(offset * offset, axis=0, keepdims=True))
    stat_tx[:, 0:C] = own_sum
    stat_tx[:, C : 2 * C] = own_squares
    pl.semaphore_wait(barrier, FRAMES - 1 + 3)

    for i, mate in enumerate(mates):
        remote(stat_tx, stat_rx.at[i], send_sem.at[0], recv_sem.at[0], clip, mate).start()

    before = lax.rem(frame + FRAMES - 2, FRAMES)
    after = lax.rem(frame + 2, FRAMES)
    for n in range(CHUNKS):
        rows = pl.ds(n * PIECE, PIECE)
        remote(
            cot.at[rows], cot4.at[2 + core, rows], send_sem.at[1], piece_sem.at[n], clip, before
        ).start()
    remote(cot, cot4.at[core], send_sem.at[2], recv_sem.at[2], clip, sibling).start()

    tell(0)
    pl.semaphore_signal(known.at[3], inc=1, device_id=(other, frame), device_id_type=MESH)

    copies[1].wait()
    for k in range(3):
        w_time_t[k] = w_time_v[k].T
    copies[4].wait()
    copies[5].wait()
    copies[2].wait()
    for p in range(3):
        for j in range(3):
            w_space_t[p, j * C : (j + 1) * C, :] = w_space_v[p, j * C : (j + 1) * C, :].T

    wait_for(stat_rx, recv_sem.at[0])
    own = stat_tx[...]
    sums = own[:, 0:C]
    squares = own[:, C : 2 * C]
    for i in range(FRAMES - 1):
        sums = sums + stat_rx[i, :, 0:C]
        squares = squares + stat_rx[i, :, C : 2 * C]
    center = sums / members
    part = POS * (C // GROUPS)
    away = own[:, 0:C] / part - center
    spread = away * away
    for i in range(FRAMES - 1):
        away = stat_rx[i, :, 0:C] / part - center
        spread = spread + away * away
    variance = (squares + part * spread) / members
    inv_std = lax.rsqrt(variance + EPSILON)

    column = lax.rem(lax.broadcasted_iota(jnp.int32, (POS, C), 0), COLS)
    normed = (clips_v[...].astype(F32) - center) * inv_std
    act = normed * gain[...] + shift[...]
    act_s[...] = act
    hidden = act / (1.0 + jnp.exp(-act))
    even, odd = by_parity(hidden.astype(BF16).T)
    first = core == 0
    h_tx[...] = jnp.where(first, odd, even)
    h_t[core] = jnp.where(first, even, odd)
    remote(h_tx, h_t.at[core], send_sem.at[3], recv_sem.at[3], clip, sibling).start()

    def pass_on(n):
        rows = pl.ds(n * PIECE, PIECE)
        wait_for(cot4.at[2 + core, rows], piece_sem.at[n])
        remote(
            cot4.at[2 + core, rows], cot4.at[2 + core, rows],
            send_sem.at[4], recv_sem.at[4], clip, sibling,
        ).start()

    for n in range(CHUNKS // 2):
        pass_on(n)

    for j in range(3):
        hcat[PAD : PAD + POS, j * C : (j + 1) * C] = shifted(hidden, j - 1, column).astype(BF16)
    mixed = dot(hcat[0:POS, :], w_space_v[0])
    for p in range(1, 3):
        mixed = mixed + dot(hcat[p * COLS : p * COLS + POS, :], w_space_v[p])
    mixed = mixed.astype(BF16)
    mixed_own[...] = mixed
    even, odd = by_parity(mixed.T)
    m_tx[...] = jnp.where(first, odd, even)
    m_t[core] = jnp.where(first, even, odd)
    remote(m_tx, m_t.at[core], send_sem.at[5], recv_sem.at[5], clip, sibling).start()

    for n in range(CHUNKS // 2, CHUNKS):
        pass_on(n)

    copies[3].wait()
    wait_for(cot4.at[0], recv_sem.at[2])
    ng_s[...] = dot(cot4[0], w_time_t[0]) + dot(cot4[1], w_time_t[1])
    hid_grad_s[...] = dot(cot4[1], w_time_t[0])
    wait_for(cot4.at[0], recv_sem.at[4])
    wait_for(cot4.at[0], send_sem.at[4])

    @pl.when(q == CHIPS - 1)
    def _():
        cot4[2] = jnp.zeros((POS, C), BF16)
        cot4[3] = jnp.zeros((POS, C), BF16)

    def scatter(tx, rx, n):
        for i, (by_x, by_y) in enumerate(PLANE_ORDER):
            x = lax.rem(2 * xh + lax.rem(q, 2) + by_x, 2 * XH)
            y = lax.rem(q // 2 + by_y, CHIPS // 2)
            xh_to, q_to = x // 2, 2 * y + lax.rem(x, 2)
            remote(
                tx.at[xh_to * CHIPS + q_to], rx.at[i], send_sem.at[n], recv_sem.at[n],
                xh_to * ZS + z, 2 * q_to + core,
            ).start()

    pl.semaphore_wait(known.at[0], 2)
    tell(1)
    wait_for(m_t.at[0], recv_sem.at[5])
    for k in range(3):
        total = (dot(m_t[0], cot4[k]) + dot(m_t[1], cot4[k + 1])).astype(BF16)
        for half in range(2):
            for to in range(CHIPS):
                rs_tx_b[half * CHIPS + to, k] = total[
                    to * 16 : to * 16 + 16, half * 128 : half * 128 + 128
                ]

    pl.semaphore_wait(known.at[3], 1)
    scatter(rs_tx_b, rs_rx_b, 7)

    for a in range(2):
        if a == 0:
            mg = ng_s[...] + dot(cot4[2], w_time_t[2])
        else:
            mg = hid_grad_s[...] + dot(cot4[2], w_time_t[1]) + dot(cot4[3], w_time_t[2])
        mg = mg.astype(BF16).astype(F32)
        for j in range(3):
            mgcat[a, PAD : PAD + POS, j * C : (j + 1) * C] = shifted(mg, 1 - j, column).astype(BF16)

    wait_for(h_t.at[0], recv_sem.at[3])
    row_groups = ((rs_tx_a, rs_rx_a, 6), (rs_tx_c, rs_rx_c, 13), (rs_tx_d, rs_rx_d, 15))
    for p, (tx, rx, n) in enumerate(row_groups):
        rows = pl.ds((2 - p) * COLS, POS)
        total = dot(h_t[0], mgcat[0, rows, :]) + dot(h_t[1], mgcat[1, rows, :])
        total = total.astype(BF16)
        for half in range(2):
            for to in range(CHIPS):
                for j in range(3):
                    tx[half * CHIPS + to, j] = total[
                        to * 16 : to * 16 + 16, j * C + half * 128 : j * C + half * 128 + 128
                    ]
        scatter(tx, rx, n)
    pl.semaphore_wait(known.at[1], 2)
    tell(2)

    hidden_grad = dot(mgcat[core, 2 * COLS : 2 * COLS + POS, :], w_space_t[0])
    for p in range(1, 3):
        rows = pl.ds((2 - p) * COLS, POS)
        hidden_grad = hidden_grad + dot(mgcat[core, rows, :], w_space_t[p])
    act = act_s[...]
    s = 1.0 / (1.0 + jnp.exp(-act))
    ng = hidden_grad * s * (1.0 + act * (1.0 - s)) * gain[...]
    ng_s[...] = ng
    normed = (clips_v[...].astype(F32) - center) * inv_std
    mean_tx[:, 0:C] = group_spread(jnp.sum(ng, axis=0, keepdims=True))
    mean_tx[:, C : 2 * C] = group_spread(jnp.sum(ng * normed, axis=0, keepdims=True))

    for i, mate in enumerate(mates):
        remote(mean_tx, mean_rx.at[i], send_sem.at[9], recv_sem.at[9], clip, mate).start()

    me = xh * CHIPS + q

    def along_z(first_tap, count):
        def send(i):
            to = lax.rem(z + ZS + far_first(i), ZS)
            for n in range(2):
                tap = lax.rem(to, HALF) + HALF * n

                @pl.when((tap >= first_tap) & (tap < first_tap + count))
                def _(n=n, tap=tap):
                    remote(
                        z_tx.at[tap], z_rx.at[n * ZS + z], send_sem.at[10], recv_sem.at[10 + 4 * n],
                        xh * ZS + to, frame,
                    ).start()

        loop(ZS - 1, send)

    def plane_sums(tx, rx, n, first_tap, count):
        wait_for(rx, recv_sem.at[n])
        for k in range(count):
            total = tx[me, k].astype(F32)
            for i in range(XH * CHIPS - 1):
                total = total + rx[i, k].astype(F32)
            z_tx[first_tap + k] = total

    plane_sums(rs_tx_b, rs_rx_b, 7, 9, 3)
    pl.semaphore_wait(known.at[2], 2)
    along_z(9, 3)
    for p, (tx, rx, n) in enumerate(row_groups):
        plane_sums(tx, rx, n, 3 * p, 3)
        along_z(3 * p, 3)

    remote(mixed_own, mixed_halo, send_sem.at[8], recv_sem.at[8], clip, after).start()

    scale = 1.0 / math.sqrt(XH * ZS * FRAMES * POS)
    rest = lax.rem(z, HALF)

    def finish(n):
        tap = rest + HALF * n
        wait_for(z_rx.at[pl.ds(0, ZS - 1)], recv_sem.at[10 + 4 * n])
        z_rx[n * ZS + z] = z_tx[tap]
        total = z_rx[n * ZS]
        for i in range(1, ZS):
            total = total + z_rx[n * ZS + i]
        done = (total * scale).astype(BF16)
        fin_tx[n] = done
        gathered[tap * 2 + xh] = done

        def hand(clip_to):
            remote(
                fin_tx.at[n], gathered.at[tap * 2 + xh], send_sem.at[12], recv_sem.at[12],
                clip_to, frame,
            ).start()

        for step in (-4, 3, -3, 2, -2, 1, -1):
            to = lax.rem(z + step + ZS, ZS)
            hand((1 - xh) * ZS + to)
            hand(xh * ZS + to)
        hand(other)

    @pl.when(rest < TAPS - HALF)
    def _():
        finish(1)

    finish(0)

    wait_for(mean_rx, recv_sem.at[9])
    both = mean_tx[...]
    for i in range(FRAMES - 1):
        both = both + mean_rx[i]
    both = both / members
    m1, m2 = both[:, 0:C], both[:, C : 2 * C]
    normed = (clips_v[...].astype(F32) - center) * inv_std
    grad_v[...] = (
        cot4[core].astype(F32) + inv_std * (ng_s[...] - m1 - normed * m2)
    ).astype(BF16)
    grad_copy = pltpu.make_async_copy(grad_v, grad_out, local_sem.at[6])
    grad_copy.start()

    wait_for(mixed_halo, recv_sem.at[8])

    @pl.when(core == 0)
    def _():
        remote(mixed_own, mixed_sib, send_sem.at[11], recv_sem.at[11], clip, sibling).start()

    @pl.when(core == 1)
    def _():
        remote(mixed_halo, mixed_sib, send_sem.at[11], recv_sem.at[11], clip, sibling).start()

    temporal = dot(mixed_own[...], w_time_v[0])
    temporal = temporal + jnp.where(q > 0, dot(mixed_halo[...], w_time_v[2]), 0.0)
    wait_for(mixed_sib, recv_sem.at[11])
    temporal = temporal + jnp.where(frame > 0, dot(mixed_sib[...], w_time_v[1]), 0.0)
    result_v[...] = (clips_v[...].astype(F32) + temporal.astype(BF16).astype(F32)).astype(BF16)
    result_copy = pltpu.make_async_copy(result_v, result_out, local_sem.at[7])
    result_copy.start()

    @pl.when(rest < TAPS - HALF)
    def _():
        wait_for(gathered.at[pl.ds(0, 2 * TAPS - 2)], recv_sem.at[12])
        wait_for(gathered.at[pl.ds(0, 2 * (ZS - 1))], send_sem.at[12])
        wait_for(z_rx.at[pl.ds(0, 2 * TAPS - 2)], send_sem.at[10])

    @pl.when(rest >= TAPS - HALF)
    def _():
        wait_for(gathered.at[pl.ds(0, 2 * TAPS - 1)], recv_sem.at[12])
        wait_for(gathered.at[pl.ds(0, ZS - 1)], send_sem.at[12])
        wait_for(z_rx.at[pl.ds(0, 2 * TAPS - 1)], send_sem.at[10])

    for k in range(TAPS):
        for half in range(2):
            taps_v[k, :, half * 128 : half * 128 + 128] = gathered[2 * k + half]
    taps_copy = pltpu.make_async_copy(taps_v, taps_out, local_sem.at[8])
    taps_copy.start()

    wait_for(stat_rx, send_sem.at[0])
    wait_for(cot4.at[0], send_sem.at[1])
    wait_for(cot4.at[0], send_sem.at[2])
    wait_for(h_tx, send_sem.at[3])
    wait_for(m_tx, send_sem.at[5])
    wait_for(rs_rx_a, send_sem.at[6])
    wait_for(rs_rx_b, send_sem.at[7])
    wait_for(rs_rx_c, send_sem.at[13])
    wait_for(rs_rx_d, send_sem.at[15])
    wait_for(mixed_own, send_sem.at[8])
    wait_for(mean_rx, send_sem.at[9])
    wait_for(mixed_own, send_sem.at[11])
    for copy in (grad_copy, result_copy, taps_copy):
        copy.wait()


def write_out(result, grad, taps, result_out, grad_out, space_out, time_out, *scratch):
    result_v, grad_v, taps_v, in_sem, out_sem = scratch
    moves = [(taps, taps_v, ((0, 9, space_out), (9, 3, time_out)))]
    for source, held, target in ((result, result_v, result_out), (grad, grad_v, grad_out)):
        moves.append((source, held, ((0, POS, target),)))
    into = [
        pltpu.make_async_copy(source, held, in_sem.at[n])
        for n, (source, held, _) in enumerate(moves)
    ]
    for copy in into:
        copy.start()
    back = []
    for copy, (_, held, parts) in zip(into, moves):
        copy.wait()
        for first, count, target in parts:
            back.append(
                pltpu.make_async_copy(held.at[pl.ds(first, count)], target, out_sem.at[len(back)])
            )
            back[-1].start()
    for copy in back:
        copy.wait()


def per_device(clips, cotangent, norm_gain, norm_shift, w_spatial, w_time):
    hbm = pl.BlockSpec(memory_space=pltpu.HBM)
    blocks = pl.pallas_call(
        kernel,
        name="video_block",
        out_shape=(
            jax.ShapeDtypeStruct((POS, C), BF16),
            jax.ShapeDtypeStruct((POS, C), BF16),
            jax.ShapeDtypeStruct((TAPS, 16, C), BF16),
        ),
        in_specs=[hbm] * 6,
        out_specs=(hbm, hbm, hbm),
        scratch_shapes=[
            pltpu.VMEM((POS, C), BF16),
            pltpu.VMEM((4, POS, C), BF16),
            pltpu.VMEM((3, 3 * C, C), BF16),
            pltpu.VMEM((3, C, C), BF16),
            pltpu.VMEM((3, 3 * C, C), BF16),
            pltpu.VMEM((3, C, C), BF16),
            pltpu.VMEM((POS + 2 * PAD, 3 * C), BF16),
            pltpu.VMEM((2, POS + 2 * PAD, 3 * C), BF16),
            pltpu.VMEM((POS, C), F32),
            pltpu.VMEM((POS, C), F32),
            pltpu.VMEM((POS, C), F32),
            pltpu.VMEM((2, 128, POS), BF16),
            pltpu.VMEM((128, POS), BF16),
            pltpu.VMEM((2, 128, POS), BF16),
            pltpu.VMEM((128, POS), BF16),
            pltpu.VMEM((POS, C), BF16),
            pltpu.VMEM((POS, C), BF16),
            pltpu.VMEM((POS, C), BF16),
            pltpu.VMEM((1, 2 * C), F32),
            pltpu.VMEM((FRAMES - 1, 1, 2 * C), F32),
            pltpu.VMEM((1, 2 * C), F32),
            pltpu.VMEM((FRAMES - 1, 1, 2 * C), F32),
            pltpu.VMEM((XH * CHIPS, 3, 16, 128), BF16),
            pltpu.VMEM((XH * CHIPS - 1, 3, 16, 128), BF16),
            pltpu.VMEM((XH * CHIPS, 3, 16, 128), BF16),
            pltpu.VMEM((XH * CHIPS - 1, 3, 16, 128), BF16),
            pltpu.VMEM((XH * CHIPS, 3, 16, 128), BF16),
            pltpu.VMEM((XH * CHIPS - 1, 3, 16, 128), BF16),
            pltpu.VMEM((XH * CHIPS, 3, 16, 128), BF16),
            pltpu.VMEM((XH * CHIPS - 1, 3, 16, 128), BF16),
            pltpu.VMEM((TAPS, 16, 128), F32),
            pltpu.VMEM((2 * ZS, 16, 128), F32),
            pltpu.VMEM((2, 16, 128), BF16),
            pltpu.VMEM((XH * ZS - 1, 16, 128), BF16),
            pltpu.VMEM((1, C), F32),
            pltpu.VMEM((1, C), F32),
            pltpu.VMEM((POS, C), BF16),
            pltpu.VMEM((POS, C), BF16),
            pltpu.VMEM((TAPS, 16, C), BF16),
            pltpu.SemaphoreType.DMA((9,)),
            pltpu.SemaphoreType.DMA((16,)),
            pltpu.SemaphoreType.DMA((16,)),
            pltpu.SemaphoreType.DMA((CHUNKS,)),
            pltpu.SemaphoreType.REGULAR((4,)),
        ],
        compiler_params=pltpu.CompilerParams(
            collective_id=0, has_side_effects=True, vmem_limit_bytes=VMEM_BYTES
        ),
    )(
        clips.reshape(POS, C),
        cotangent.reshape(POS, C),
        norm_gain.reshape(1, C),
        norm_shift.reshape(1, C),
        w_spatial.reshape(3, 3 * C, C),
        w_time,
    )
    result, grad, space, time = pl.pallas_call(
        write_out,
        name="write_out",
        out_shape=(
            jax.ShapeDtypeStruct((POS, C), BF16),
            jax.ShapeDtypeStruct((POS, C), BF16),
            jax.ShapeDtypeStruct((9, 16, C), BF16),
            jax.ShapeDtypeStruct((3, 16, C), BF16),
        ),
        in_specs=[hbm, hbm, hbm],
        out_specs=(hbm, hbm, hbm, hbm),
        scratch_shapes=[
            pltpu.VMEM((POS, C), BF16),
            pltpu.VMEM((POS, C), BF16),
            pltpu.VMEM((TAPS, 16, C), BF16),
            pltpu.SemaphoreType.DMA((5,)),
            pltpu.SemaphoreType.DMA((6,)),
        ],
        compiler_params=pltpu.CompilerParams(vmem_limit_bytes=VMEM_BYTES),
    )(*blocks)
    return (
        result.reshape(clips.shape),
        grad.reshape(clips.shape),
        space.reshape(3, 3, 16, C),
        time,
    )


def solution(mesh):
    placed = (
        P("clip", "frame", None, None, None),
        P("clip", "frame", None, None, None),
        P(),
        P(),
        P(),
        P(),
    )
    return jax.shard_map(
        per_device,
        mesh=mesh,
        in_specs=placed,
        out_specs=(
            P("clip", "frame", None, None, None),
            P("clip", "frame", None, None, None),
            P(None, None, "frame", None),
            P(None, "frame", None),
        ),
        check_vma=False,
    )
```
